512 devices in a mesh: section: 8 (over z_lo, x), expert: 64 (over z_hi, y, core).
Axes of the slice: x: 4, y: 8, z: 8 (z_hi: 4, z_lo: 2; z = z_hi * 2 + z_lo), core: 2. Of those that a mesh axis runs over, the one named last changes fastest.
Arguments:
- fwd_act: bfloat16 [8, 8192, 2048], P('section', 'expert'), may hold values from -6 to 6
- fwd_ids: int32 [8, 8192, 8], P('section', 'expert'), may hold values from 0 to 127, all different within a row; in each aligned block of 128 rows (0 to 127, 128 to 255, ..., all dimensions but the last counted through in order) at most 10 rows name the same one
- fwd_gates: float32 [8, 8192, 8], P('section', 'expert'), may hold values from 0.1 to 1
- bwd_input: bfloat16 [8, 8192, 2048], P('section', 'expert'), may hold values from -6 to 6
- bwd_ids: int32 [8, 8192, 8], P('section', 'expert'), may hold values from 0 to 127, all different within a row; in each aligned block of 128 rows (0 to 127, 128 to 255, ..., all dimensions but the last counted through in order) at most 10 rows name the same one
- bwd_gates: float32 [8, 8192, 8], P('section', 'expert'), may hold values from 0.1 to 1
- bwd_grad: bfloat16 [8, 8192, 2048], P('section', 'expert'), may hold values from -6 to 6
- w_gate: bfloat16 [8, 2048, 12288], P('section', None, 'expert'), may hold values from -0.125 to 0.125
- w_up: bfloat16 [8, 2048, 12288], P('section', None, 'expert'), may hold values from -0.125 to 0.125
- w_down: bfloat16 [8, 12288, 2048], P('section', 'expert'), may hold values from -0.21875 to 0.21875
Outputs:
- routed_out: bfloat16 [8, 8192, 2048], P('section', 'expert')
- input_grad: bfloat16 [8, 8192, 2048], P('section', 'expert')
The draws below stay inside these ranges and needn't reach their ends.
Inputs may be any that keep to these rules, and one draw needn't show every extreme that they name: `fwd_ids`: each row names 8 different experts; among the 128 rows of one device no expert is named more than 10 times. `bwd_ids`: each row names 8 different experts; among the 128 rows of one device no expert is named more than 10 times.
All inputs are finite; a program needn't handle non-finite values.
Results may differ from the reference program's by a relative error of at most 0.0064.
Values may be sent and summed in bfloat16 or wider, within the bound.
No kernel may reach another device: no remote copies, remote signals or barrier semaphores. Data moves between devices by JAX's collectives and lax.ppermute only.
A program may use at most 128 MiB of HBM per device.

```python
import math
import jax
import jax.numpy as jnp
import numpy as np
from jax import lax

D = 2048
HIDDEN_SIZE = 768
EXPERTS_ALL = 128
TOP = 8
SHARDS = 4
TOK_DEV = 128
HDEV = 192
EXP_WIN = 16
CAP = 10
TOKENS = 8192
LAYERS = 8
N_EXPERT = 64


def shard_levels(own_key, dims, cuts, least, largest):
    factor_of = 1.0
    for axis_at, shards_of in cuts:
        draws = jax.random.uniform(jax.random.fold_in(jax.random.fold_in(own_key, 6), axis_at), (shards_of,), jnp.float32, least / len(cuts), largest / len(cuts))
        factor_of = factor_of * jnp.repeat(jnp.exp(draws), dims[axis_at] // shards_of).reshape((-1,) + (1,) * (len(dims) - 1 - axis_at))
    return factor_of


def assign_block(rng, own, number, rows, amount, top, reach, skew):
    sequence = jax.random.permutation(rng, amount)
    packed, common = shares(amount, rows * top, reach, skew, True), shares(amount, rows * top, reach, skew, False)
    places = jnp.arange(amount)

    def named(lengths, rotation):
        used = int((lengths > 0).sum())
        fixed = max(1, used // 4)
        passed = fixed + (places - fixed + rotation * (used - fixed)) % max(1, amount - fixed)
        return jnp.zeros((amount,), jnp.int32).at[sequence[jnp.where(places < fixed, places, passed)]].set(jnp.asarray(lengths, jnp.int32))

    lengths = jnp.where(number % 4 == 0, named(packed, number // 4), named(common, number - number // 4 - 1))
    mixed = jax.random.permutation(jax.random.fold_in(own, 3), amount)
    source_of, taker = mixed[0:amount // 2 * 2:2], mixed[1:amount // 2 * 2:2]
    room = jnp.minimum(lengths[source_of] - 1, reach - lengths[taker]) // 2
    room = jnp.where((source_of == sequence[0]) | (taker == sequence[0]) | (lengths[taker] == 0), 0, jnp.maximum(room, 0))
    passed = jax.random.randint(jax.random.fold_in(own, 4), (amount // 2,), 0, 1 << 20) % (room + 1)
    lengths = lengths.at[source_of].add(-passed).at[taker].add(passed)
    items = jnp.searchsorted(jnp.cumsum(lengths), jnp.arange(rows * top), side="right").astype(jnp.int32)
    grid = items.reshape(top, rows).T
    grid = grid[jax.random.permutation(jax.random.fold_in(own, 1), rows)]
    rotation = jax.random.randint(jax.random.fold_in(own, 2), (rows, 1), 0, top)
    return jnp.take_along_axis(grid, (jnp.arange(top)[None, :] + rotation) % top, axis=1)


def shares(number_of, total, reach, slope, full):
    loads = [(1 << 20) // math.isqrt(rank ** slope) + 1 for rank in range(1, number_of + 1)]
    largest = reach if full else min(reach, max(-(-total // number_of), total * loads[0] // sum(loads)))
    least = 1 if total - largest >= number_of - 1 else 0
    counts, rest = [largest] + [least] * (number_of - 1), total - largest - least * (number_of - 1)
    while rest > 0:
        movable = [i for i in range(1, number_of) if counts[i] < largest] or [i for i in range(1, number_of) if counts[i] < reach]
        pool, budget = sum([loads[i] for i in movable]), rest
        for i in movable:
            extra = min(reach - counts[i], max(1, budget * loads[i] // pool), rest)
            counts[i] = counts[i] + extra
            rest = rest - extra
    return np.array(counts)


def centred(own_key, dims, deviation, limit, shards=(), held_as=jnp.bfloat16):
    entries = deviation * jax.random.normal(own_key, dims, jnp.float32)
    if shards:
        entries = entries * shard_levels(own_key, dims, shards, -0.22, 0.18)
    return jnp.clip(entries, -limit, limit).astype(held_as)


def setup_inputs(seed: int = 0) -> dict:
    splits = jax.random.split(jax.random.key(seed), 11)
    fwd_act = centred(splits[0], (LAYERS, TOKENS, D), 1.0, 6.0, ((0, 8), (1, 64)))
    fwd_ids_keys = jax.random.split(jax.random.fold_in(splits[1], 1), LAYERS * TOKENS // TOK_DEV)
    fwd_ids_turns = jax.random.permutation(jax.random.fold_in(splits[1], 3), LAYERS * TOKENS // TOK_DEV)
    fwd_ids = jax.vmap(lambda own, number: assign_block(jax.random.fold_in(splits[1], 2), own, number, TOK_DEV, EXPERTS_ALL, TOP, CAP, 2))(fwd_ids_keys, fwd_ids_turns).reshape((LAYERS, TOKENS, TOP))
    fwd_gates = jnp.clip(jnp.exp(math.log(1.0) - 2.3025851 * jax.random.uniform(splits[2], (LAYERS, TOKENS, TOP), jnp.float32) ** shard_levels(splits[2], (LAYERS, TOKENS, TOP), ((0, 8), (1, 64)), -0.2, 0.2)), 0.1, 1.0)
    bwd_input = centred(splits[3], (LAYERS, TOKENS, D), 1.0, 6.0, ((0, 8), (1, 64)))
    bwd_ids_keys = jax.random.split(jax.random.fold_in(splits[4], 1), LAYERS * TOKENS // TOK_DEV)
    bwd_ids_turns = jax.random.permutation(jax.random.fold_in(splits[4], 3), LAYERS * TOKENS // TOK_DEV)
    bwd_ids = jax.vmap(lambda own, number: assign_block(jax.random.fold_in(splits[4], 2), own, number, TOK_DEV, EXPERTS_ALL, TOP, CAP, 2))(bwd_ids_keys, bwd_ids_turns).reshape((LAYERS, TOKENS, TOP))
    bwd_gates = jnp.clip(jnp.exp(math.log(1.0) - 2.3025851 * jax.random.uniform(splits[5], (LAYERS, TOKENS, TOP), jnp.float32) ** shard_levels(splits[5], (LAYERS, TOKENS, TOP), ((0, 8), (1, 64)), -0.2, 0.2)), 0.1, 1.0)
    bwd_grad = centred(splits[6], (LAYERS, TOKENS, D), 1.0, 6.0, ((0, 8), (1, 64)))
    w_gate = centred(splits[7], (LAYERS, D, EXP_WIN * HIDDEN_SIZE), D ** -0.5, 0.125, ((0, 8), (2, 64)))
    w_up = centred(splits[8], (LAYERS, D, EXP_WIN * HIDDEN_SIZE), D ** -0.5, 0.125, ((0, 8), (2, 64)))
    w_down = centred(splits[9], (LAYERS, EXP_WIN * HIDDEN_SIZE, D), HIDDEN_SIZE ** -0.5, 0.21875, ((0, 8), (1, 64)))
    return {"fwd_act": fwd_act, "fwd_ids": fwd_ids, "fwd_gates": fwd_gates, "bwd_input": bwd_input, "bwd_ids": bwd_ids, "bwd_gates": bwd_gates, "bwd_grad": bwd_grad, "w_gate": w_gate, "w_up": w_up, "w_down": w_down}


def slot_tables(route_ids, route_gates):
    local_rows = route_ids.shape[0]
    per_token = route_ids.shape[1]
    flat_ids = route_ids.reshape(-1)
    chosen = (flat_ids[:, None] == jnp.arange(EXP_WIN, dtype=jnp.int32)[None, :]).astype(jnp.int32)
    before = jnp.cumsum(chosen, axis=0) - chosen
    slot_of = jnp.sum(before * chosen, axis=1).astype(jnp.int32)
    expert_safe = jnp.where(flat_ids < EXP_WIN, flat_ids, EXP_WIN).astype(jnp.int32)
    token_of = (jnp.arange(local_rows * per_token, dtype=jnp.int32) // per_token).astype(jnp.int32)
    table = jnp.full((EXP_WIN + 1, CAP), local_rows, jnp.int32).at[expert_safe, slot_of].set(token_of)
    weights = jnp.zeros((EXP_WIN + 1, CAP), jnp.float32).at[expert_safe, slot_of].set(route_gates.reshape(-1))
    return table[:EXP_WIN], weights[:EXP_WIN]


def expert_rows(route_ids, route_gates):
    tables, weights = jax.vmap(slot_tables)(route_ids.reshape(N_EXPERT, TOK_DEV, TOP), route_gates.reshape(N_EXPERT, TOK_DEV, TOP))
    offsets = (jnp.arange(N_EXPERT, dtype=jnp.int32) * TOK_DEV)[:, None, None]
    global_rows = jnp.where(tables < TOK_DEV, tables + offsets, TOKENS).astype(jnp.int32)
    global_rows = jnp.transpose(global_rows, (1, 0, 2)).reshape(EXP_WIN, N_EXPERT * CAP)
    weights = jnp.transpose(weights, (1, 0, 2)).reshape(EXP_WIN, N_EXPERT * CAP)
    return global_rows, weights


def split_weights(gate_all, up_all, down_all):
    gate_each = jnp.transpose(gate_all.reshape(D, EXP_WIN, HIDDEN_SIZE), (1, 0, 2))
    up_each = jnp.transpose(up_all.reshape(D, EXP_WIN, HIDDEN_SIZE), (1, 0, 2))
    down_each = down_all.reshape(EXP_WIN, HIDDEN_SIZE, D)
    return gate_each, up_each, down_each


def with_zero_row(states):
    return jnp.concatenate([states, jnp.zeros((1, D), states.dtype)], axis=0)


def back_to_float(values):
    return lax.optimization_barrier(values.astype(jnp.bfloat16)).astype(jnp.float32)


def forward_section(states, route_ids, route_gates, gate_all, up_all, down_all):
    global_rows, weights = expert_rows(route_ids, route_gates)
    gathered = with_zero_row(states)[global_rows]
    gate_each, up_each, down_each = split_weights(gate_all, up_all, down_all)

    def one_expert(pieces):
        rows_in, gate_w, up_w, down_w = pieces
        gate_pre = jnp.dot(rows_in, gate_w, preferred_element_type=jnp.float32)
        up_pre = jnp.dot(rows_in, up_w, preferred_element_type=jnp.float32)
        act = (jax.nn.silu(gate_pre) * up_pre).astype(jnp.bfloat16)
        total = jnp.zeros((rows_in.shape[0], D), jnp.float32)
        for group in range(SHARDS):
            lower = group * HDEV
            part = jnp.dot(act[:, lower:lower + HDEV], down_w[lower:lower + HDEV], preferred_element_type=jnp.float32)
            total = total + back_to_float(part)
        return total

    summed = lax.map(one_expert, (gathered, gate_each, up_each, down_each))
    weighted = (weights[:, :, None] * summed).reshape(-1, D)
    result = jnp.zeros((TOKENS + 1, D), jnp.float32).at[global_rows.reshape(-1)].add(weighted)
    return result[:TOKENS].astype(jnp.bfloat16)


def backward_section(states, route_ids, route_gates, incoming, gate_all, up_all, down_all):
    global_rows, weights = expert_rows(route_ids, route_gates)
    gathered = with_zero_row(states)[global_rows]
    grad_rows = with_zero_row(incoming)[global_rows]
    scaled = (grad_rows.astype(jnp.float32) * weights[:, :, None]).astype(jnp.bfloat16)
    gate_each, up_each, down_each = split_weights(gate_all, up_all, down_all)

    def one_expert(pieces):
        rows_in, scaled_rows, gate_w, up_w, down_w = pieces
        gate_back = jnp.dot(rows_in, gate_w, preferred_element_type=jnp.float32)
        up_back = jnp.dot(rows_in, up_w, preferred_element_type=jnp.float32)
        dact = jnp.dot(scaled_rows, down_w.T, preferred_element_type=jnp.float32)
        sigma = jax.nn.sigmoid(gate_back)
        dgate = (dact * up_back * sigma * (1.0 + gate_back * (1.0 - sigma))).astype(jnp.bfloat16)
        dup = (dact * jax.nn.silu(gate_back)).astype(jnp.bfloat16)
        total = jnp.zeros((rows_in.shape[0], D), jnp.float32)
        for group in range(SHARDS):
            lower = group * HDEV
            part = jnp.dot(dgate[:, lower:lower + HDEV], gate_w[:, lower:lower + HDEV].T, preferred_element_type=jnp.float32)
            part = part + jnp.dot(dup[:, lower:lower + HDEV], up_w[:, lower:lower + HDEV].T, preferred_element_type=jnp.float32)
            total = total + back_to_float(part)
        return total

    summed = lax.map(one_expert, (gathered, scaled, gate_each, up_each, down_each))
    result = jnp.zeros((TOKENS + 1, D), jnp.float32).at[global_rows.reshape(-1)].add(summed.reshape(-1, D))
    return result[:TOKENS].astype(jnp.bfloat16)


def reference(fwd_act, fwd_ids, fwd_gates, bwd_input, bwd_ids, bwd_gates, bwd_grad, w_gate, w_up, w_down):
    inbound = jnp.concatenate([fwd_act[:1], fwd_act[:-1]], axis=0)
    grads = jnp.concatenate([bwd_grad[1:], bwd_grad[-1:]], axis=0)

    def forward_one(pieces):
        return forward_section(*pieces)

    def backward_one(pieces):
        return backward_section(*pieces)

    routed_out = lax.map(forward_one, (inbound, fwd_ids, fwd_gates, w_gate, w_up, w_down))
    input_grad = lax.map(backward_one, (bwd_input, bwd_ids, bwd_gates, grads, w_gate, w_up, w_down))
    return routed_out, input_grad
```

```python
import functools

import jax
import jax.numpy as jnp
from jax import lax
from jax.experimental import pallas as pl
from jax.experimental.pallas import tpu as pltpu
from jax.sharding import Mesh
from jax.sharding import PartitionSpec as P

EXPERTS = 16
SHARDS = 4
CAP = 10
TILE = 16
CHUNKS = 8
ROWS = EXPERTS * CAP
SPAN = EXPERTS * TILE
PACKED = CAP * CHUNKS
TILES = PACKED // TILE
NONE = -100.0

MEETS = [
    (j, c, TILE * j - CAP * c)
    for j in range(TILES)
    for c in range(CHUNKS)
    if -TILE < TILE * j - CAP * c < CAP
]

BF16 = jnp.bfloat16
F32 = jnp.float32
NT = (((1,), (1,)), ((), ()))
VMEM = pl.BlockSpec(memory_space=pltpu.VMEM)
SMEM = pl.BlockSpec(memory_space=pltpu.SMEM)


def iota(shape, dim):
    return lax.broadcasted_iota(jnp.int32, shape, dim)


def dot(a, b):
    return jnp.dot(a, b, preferred_element_type=F32)


def dot_nt(a, b):
    return lax.dot_general(a, b, NT, preferred_element_type=F32)


def halves(values):
    upper = values.astype(BF16)
    return upper, (values - upper.astype(F32)).astype(BF16)


def call(body, outs, n_in, scratch=(), smem=0, flops=0, size=0, vmem=40):
    return pl.pallas_call(
        body,
        out_shape=outs,
        in_specs=[SMEM] * smem + [VMEM] * (n_in - smem),
        out_specs=jax.tree.map(lambda _: VMEM, outs),
        scratch_shapes=list(scratch),
        compiler_params=pltpu.CompilerParams(vmem_limit_bytes=vmem * 2**20),
        cost_estimate=pl.CostEstimate(flops=flops, bytes_accessed=size, transcendentals=0),
    )


def keys_by_expert(ids, gates, turn):
    tokens, top = ids.shape
    turn[:, :top] = ids.astype(F32)
    turn[:, top : 2 * top] = gates
    turned = turn[...].T
    expert = iota((EXPERTS, tokens), 0).astype(F32)
    chosen = jnp.zeros((EXPERTS, tokens), F32)
    gate = jnp.zeros((EXPERTS, tokens), F32)
    for k in range(top):
        hit = turned[k : k + 1] == expert
        chosen = chosen + hit.astype(F32)
        gate = gate + jnp.where(hit, turned[top + k : top + k + 1], 0.0)
    earlier = (iota((tokens, tokens), 0) < iota((tokens, tokens), 1)).astype(F32).astype(BF16)
    slot = dot(chosen.astype(BF16), earlier)
    return jnp.where(chosen > 0, slot, NONE), gate


def spread_rows(values):
    experts, tokens = values.shape
    wide = jnp.broadcast_to(values[:, None, :], (experts, TILE, tokens))
    return wide.reshape(experts * TILE, tokens)


def pick_body(weighted, *refs):
    if weighted is None:
        ids, gates, own, out, turn = refs
        states = own
    else:
        edge, ids, gates, own, shifted, out, turn, states = refs
        at_edge = edge[0] == 1

        @pl.when(at_edge)
        def _():
            states[...] = own[...]

        @pl.when(jnp.logical_not(at_edge))
        def _():
            states[...] = shifted[...]

    key, gate = keys_by_expert(ids[...], gates[...], turn)
    key = spread_rows(key)
    row = lax.rem(iota(key.shape, 0), TILE).astype(F32)
    parts = [1.0]
    if weighted:
        parts = [h.astype(F32) for h in halves(spread_rows(gate))]
    width = own.shape[1] // CHUNKS
    for j in range(TILES):
        total = jnp.zeros((SPAN, width), F32)
        for _, c, shift in [m for m in MEETS if m[0] == j]:
            hit = key == row + float(shift)
            piece = states[:, c * width : (c + 1) * width]
            for part in parts:
                total = total + dot(jnp.where(hit, part, 0.0).astype(BF16), piece)
        out[:, j * TILE : (j + 1) * TILE, :] = total.astype(BF16).reshape(EXPERTS, TILE, width)


def pick(ids, gates, own, shifted=None, edge=None, weighted=False):
    tokens, width = own.shape
    out = jax.ShapeDtypeStruct((EXPERTS, PACKED, width // CHUNKS), BF16)
    scratch = [pltpu.VMEM((tokens, 128), F32)]
    cost = {"flops": 400_000_000, "size": 2_000_000}
    if shifted is None:
        return call(functools.partial(pick_body, None), out, 3, scratch, **cost)(ids, gates, own)
    scratch.append(pltpu.VMEM((tokens, width), BF16))
    return call(functools.partial(pick_body, weighted), out, 5, scratch, smem=1, **cost)(
        edge, ids, gates, own, shifted
    )


def combine_body(weighted, ids, gates, back, out):
    tokens, top = ids.shape
    lane = iota((tokens, 128), 1)
    chosen = jnp.zeros((tokens, 128), F32)
    gate = jnp.zeros((tokens, 128), F32)
    for k in range(top):
        hit = ids[:, k : k + 1] == lane
        chosen = chosen + hit.astype(F32)
        gate = gate + jnp.where(hit, gates[:, k : k + 1], 0.0)
    earlier = (iota((tokens, tokens), 1) < iota((tokens, tokens), 0)).astype(F32).astype(BF16)
    slot = dot(earlier, chosen.astype(BF16))
    key = jnp.where(chosen > 0, slot, NONE)
    widen = (iota((128, SPAN), 0) == iota((128, SPAN), 1) // TILE).astype(F32).astype(BF16)
    key = dot(key.astype(BF16), widen)
    row = lax.rem(iota(key.shape, 1), TILE).astype(F32)
    parts = [1.0]
    if weighted:
        parts = [dot(h, widen) for h in halves(gate)]
    width = out.shape[1] // CHUNKS
    for c in range(CHUNKS):
        total = jnp.zeros((tokens, width), F32)
        for j, _, shift in [m for m in MEETS if m[1] == c]:
            hit = key == row + float(shift)
            rows = back[:, j * TILE : (j + 1) * TILE, :].reshape(SPAN, width)
            for part in parts:
                total = total + dot(jnp.where(hit, part, 0.0).astype(BF16), rows)
        out[:, c * width : (c + 1) * width] = total.astype(BF16)


def combine(ids, gates, back, weighted):
    tokens = ids.shape[0]
    out = jax.ShapeDtypeStruct((tokens, back.shape[2] * CHUNKS), BF16)
    body = functools.partial(combine_body, weighted)
    return call(body, out, 3, flops=400_000_000, size=2_000_000)(ids, gates, back)


def line_up_body(gate, up, down, out):
    hidden = gate.shape[1]
    same = (iota((hidden, hidden), 0) == iota((hidden, hidden), 1)).astype(F32).astype(BF16)
    out[0] = dot_nt(same, gate[...]).astype(BF16)
    out[1] = dot_nt(same, up[...]).astype(BF16)
    out[2] = down[...]


def line_up(gate, up, down):
    out = jax.ShapeDtypeStruct((3,) + down.shape, BF16)
    return call(line_up_body, out, 3, flops=400_000_000, size=5_000_000)(gate, up, down)


def unpack_rows(packed, rows):
    width = packed.shape[2]
    at = iota((ROWS, SPAN), 0)
    lane = iota((ROWS, SPAN), 1)
    source, line = lane // TILE, lax.rem(lane, TILE)
    for c in range(CHUNKS):
        total = jnp.zeros((ROWS, width), F32)
        for j, _, shift in [m for m in MEETS if m[1] == c]:
            slot = line + shift
            hit = (at == source * CAP + slot) & (slot >= 0) & (slot < CAP)
            tile = packed[:, j * TILE : (j + 1) * TILE, :].reshape(SPAN, width)
            total = total + dot(hit.astype(F32).astype(BF16), tile)
        rows[:, c * width : (c + 1) * width] = total.astype(BF16)


def pack_rows(rows, packed):
    width = packed.shape[2]
    at = iota((SPAN, ROWS), 1)
    place = iota((SPAN, ROWS), 0)
    source, line = place // TILE, lax.rem(place, TILE)
    for j in range(TILES):
        total = jnp.zeros((SPAN, width), F32)
        for _, c, shift in [m for m in MEETS if m[0] == j]:
            slot = line + shift
            hit = (at == source * CAP + slot) & (slot >= 0) & (slot < CAP)
            piece = rows[:, c * width : (c + 1) * width].astype(BF16)
            total = total + dot(hit.astype(F32).astype(BF16), piece)
        packed[:, j * TILE : (j + 1) * TILE, :] = total.astype(BF16).reshape(EXPERTS, TILE, width)


def forward_body(*refs):
    got, weights, out, rows, total = refs[0], refs[1 : 1 + SHARDS], *refs[1 + SHARDS :]
    unpack_rows(got, rows)
    for n, w in enumerate(weights):
        gate_pre = dot_nt(rows[...], w[0])
        up_pre = dot_nt(rows[...], w[1])
        act = (gate_pre / (1.0 + jnp.exp(-gate_pre)) * up_pre).astype(BF16)
        part = dot(act, w[2])
        total[...] = part if n == 0 else total[...] + part
    pack_rows(total, out)


def backward_body(*refs):
    got, got_scaled, weights = refs[0], refs[1], refs[2 : 2 + SHARDS]
    out, rows, scaled, total = refs[2 + SHARDS :]
    unpack_rows(got, rows)
    unpack_rows(got_scaled, scaled)
    for n, w in enumerate(weights):
        gate_back = dot_nt(rows[...], w[0])
        up_back = dot_nt(rows[...], w[1])
        dact = dot_nt(scaled[...], w[2])
        sigma = 1.0 / (1.0 + jnp.exp(-gate_back))
        dgate = (dact * up_back * sigma * (1.0 + gate_back * (1.0 - sigma))).astype(BF16)
        dup = (dact * (gate_back * sigma)).astype(BF16)
        part = dot(dgate, w[0]) + dot(dup, w[1])
        total[...] = part if n == 0 else total[...] + part
    pack_rows(total, out)


def experts_of(body, got, weights):
    width = got[0].shape[2] * CHUNKS
    scratch = [pltpu.VMEM((ROWS, width), BF16) for _ in got] + [pltpu.VMEM((ROWS, width), F32)]
    out = jax.ShapeDtypeStruct(got[0].shape, BF16)
    return call(
        body, out, len(got) + len(weights), scratch, flops=4_000_000_000, size=12_000_000
    )(*got, *weights)


def from_behind(x, axis, by):
    devices = lax.axis_size(axis)
    pairs = [(i, i + by) for i in range(devices) if 0 <= i + by < devices]
    return lax.ppermute(x, axis, pairs)


def swap(x, axis):
    return lax.ppermute(x, axis, [(0, 1), (1, 0)])


def exchange(x):
    return lax.all_to_all(x, ("plane", "pair"), split_axis=0, concat_axis=0, tiled=True)


def shards(
    fwd_act, fwd_ids, fwd_gates, bwd_input, bwd_ids, bwd_gates, bwd_grad, w_gate, w_up, w_down
):
    section_at = lax.axis_index("section")
    sections = lax.axis_size("section")
    first = (section_at == 0).astype(jnp.int32).reshape(1)
    last = (section_at == sections - 1).astype(jnp.int32).reshape(1)
    arriving = from_behind(bwd_grad[0], "section", -1)
    shifted = from_behind(fwd_act[0], "section", 1)

    own = line_up(w_gate[0], w_up[0], w_down[0])
    across = swap(own, "half")
    weights = [own, swap(own, "core"), across, swap(across, "core")]

    bwd_got = exchange(pick(bwd_ids[0], bwd_gates[0], bwd_input[0]))
    scaled_got = exchange(
        pick(bwd_ids[0], bwd_gates[0], bwd_grad[0], arriving, last, weighted=True)
    )
    fwd_got = exchange(pick(fwd_ids[0], fwd_gates[0], fwd_act[0], shifted, first))

    bwd_back = exchange(experts_of(backward_body, [bwd_got, scaled_got], weights))
    fwd_back = exchange(experts_of(forward_body, [fwd_got], weights))
    input_grad = combine(bwd_ids[0], bwd_gates[0], bwd_back, False)
    routed_out = combine(fwd_ids[0], fwd_gates[0], fwd_back, True)
    return (routed_out[None], input_grad[None])


def solution(mesh):
    sections, devices = mesh.devices.shape
    planes = 4
    parted = Mesh(
        mesh.devices.reshape(sections, planes, devices // planes // 4, 2, 2),
        ("section", "plane", "pair", "half", "core"),
    )
    expert = ("plane", "pair", "half", "core")
    rows = P("section", expert, None)
    columns = P("section", None, expert)
    return jax.shard_map(
        shards,
        mesh=parted,
        in_specs=(rows,) * 7 + (columns, columns, rows),
        out_specs=(rows, rows),
        check_vma=False,
    )
```

```python
import functools

import jax
import jax.numpy as jnp
from jax import lax
from jax.experimental import pallas as pl
from jax.experimental.pallas import tpu as pltpu
from jax.sharding import Mesh
from jax.sharding import PartitionSpec as P

EXPERTS = 16
SHARDS = 4
CAP = 10
TILE = 16
CHUNKS = 8
ROWS = EXPERTS * CAP
SPAN = EXPERTS * TILE
PACKED = CAP * CHUNKS
TILES = PACKED // TILE
NONE = -100.0

BWD, SCALED, FWD = 0, 1, 2
BWD_BACK, FWD_BACK = 0, 1

MEETS = [
    (j, c, TILE * j - CAP * c)
    for j in range(TILES)
    for c in range(CHUNKS)
    if -TILE < TILE * j - CAP * c < CAP
]

BF16 = jnp.bfloat16
F32 = jnp.float32
NT = (((1,), (1,)), ((), ()))
HBM = pl.BlockSpec(memory_space=pltpu.HBM)
SMEM = pl.BlockSpec(memory_space=pltpu.SMEM)


def iota(shape, dim):
    return lax.broadcasted_iota(jnp.int32, shape, dim)


def dot(a, b):
    return jnp.dot(a, b, preferred_element_type=F32)


def dot_nt(a, b):
    return lax.dot_general(a, b, NT, preferred_element_type=F32)


def halves(values):
    upper = values.astype(BF16)
    return upper, (values - upper.astype(F32)).astype(BF16)


def cost(flops, size):
    return pl.CostEstimate(flops=flops, bytes_accessed=size, transcendentals=0)


def keys_by_expert(ids, gates):
    top, tokens = ids.shape
    expert = iota((EXPERTS, tokens), 0)
    chosen = jnp.zeros((EXPERTS, tokens), F32)
    gate = jnp.zeros((EXPERTS, tokens), F32)
    for k in range(top):
        hit = ids[k : k + 1, :] == expert
        chosen = chosen + hit.astype(F32)
        gate = gate + jnp.where(hit, gates[k : k + 1, :], 0.0)
    earlier = (iota((tokens, tokens), 0) < iota((tokens, tokens), 1)).astype(F32).astype(BF16)
    slot = dot(chosen.astype(BF16), earlier)
    return jnp.where(chosen > 0, slot, NONE), gate


def spread_rows(values):
    experts, tokens = values.shape
    wide = jnp.broadcast_to(values[:, None, :], (experts, TILE, tokens))
    return wide.reshape(experts * TILE, tokens)


def pick_rows(key, gate, states, out):
    key = spread_rows(key)
    row = lax.rem(iota(key.shape, 0), TILE).astype(F32)
    parts = [1.0]
    if gate is not None:
        parts = [h.astype(F32) for h in halves(spread_rows(gate))]
    width = states.shape[1] // CHUNKS
    for j in range(TILES):
        total = jnp.zeros((SPAN, width), F32)
        for _, c, shift in [m for m in MEETS if m[0] == j]:
            hit = key == row + float(shift)
            piece = states[:, c * width : (c + 1) * width]
            for part in parts:
                total = total + dot(jnp.where(hit, part, 0.0).astype(BF16), piece)
        out[:, j * TILE : (j + 1) * TILE, :] = total.astype(BF16).reshape(EXPERTS, TILE, width)


def pick_body(edges, bwd_ids, bwd_gates, fwd_ids, fwd_gates, *refs):
    bwd_input, bwd_grad, arriving, fwd_act, shifted = refs[:5]
    out, states, packed, read, written = refs[-5:]

    def fetch(source, n):
        return pltpu.make_async_copy(source, states.at[n], read.at[n])

    def fetch_one_of(edge, own, moved, n):
        @pl.when(edge == 1)
        def _():
            fetch(own, n).start()

        @pl.when(edge != 1)
        def _():
            fetch(moved, n).start()

    def store(n):
        lines = pl.ds(n * PACKED, PACKED)
        return pltpu.make_async_copy(packed.at[n], out.at[:, lines, :], written.at[n])

    fetch(bwd_input, BWD).start()
    fetch_one_of(edges[1], bwd_grad, arriving, SCALED)
    fetch_one_of(edges[0], fwd_act, shifted, FWD)
    bwd_key, bwd_gate = keys_by_expert(bwd_ids, bwd_gates)
    fwd_key, _ = keys_by_expert(fwd_ids, fwd_gates)
    for n, key, gate in (
        (BWD, bwd_key, None),
        (SCALED, bwd_key, bwd_gate),
        (FWD, fwd_key, None),
    ):
        fetch(bwd_input, n).wait()
        pick_rows(key, gate, states.at[n], packed.at[n])
        store(n).start()
    for n in (BWD, SCALED, FWD):
        store(n).wait()


def pick(edges, routes, states, after):
    tokens, width = states[0].shape
    out = (EXPERTS, 3 * PACKED, width // CHUNKS)
    return pl.pallas_call(
        pick_body,
        out_shape=jax.ShapeDtypeStruct(out, BF16),
        in_specs=[SMEM] + [pl.BlockSpec()] * 4 + [HBM] * (len(states) + len(after)),
        out_specs=HBM,
        scratch_shapes=[
            pltpu.VMEM((3, tokens, width), BF16),
            pltpu.VMEM((3, EXPERTS, PACKED, width // CHUNKS), BF16),
            pltpu.SemaphoreType.DMA((3,)),
            pltpu.SemaphoreType.DMA((3,)),
        ],
        compiler_params=pltpu.CompilerParams(vmem_limit_bytes=60 * 2**20),
        cost_estimate=cost(1_600_000_000, 5_000_000),
    )(edges, *routes, *states, *after)


def combine_rows(weighted, ids, gates, back, base, out, turn):
    tokens = out.shape[0]
    key, gate = keys_by_expert(ids, gates)
    turn[:EXPERTS] = key
    turn[EXPERTS : 2 * EXPERTS] = gate
    turn[2 * EXPERTS :] = jnp.zeros((128 - 2 * EXPERTS, tokens), F32)
    turned = turn[...].T
    column, source = iota((128, SPAN), 0), iota((128, SPAN), 1) // TILE
    key = dot(turned.astype(BF16), (column == source).astype(F32).astype(BF16))
    widen = (column == source + EXPERTS).astype(F32).astype(BF16)
    row = lax.rem(iota(key.shape, 1), TILE).astype(F32)
    parts = [1.0]
    if weighted:
        parts = [dot(h, widen) for h in halves(turned)]
    width = out.shape[1] // CHUNKS
    for c in range(CHUNKS):
        total = jnp.zeros((tokens, width), F32)
        for j, _, shift in [m for m in MEETS if m[1] == c]:
            hit = key == row + float(shift)
            lines = slice(base + j * TILE, base + (j + 1) * TILE)
            rows = back[:, lines, :].reshape(SPAN, width)
            for part in parts:
                total = total + dot(jnp.where(hit, part, 0.0).astype(BF16), rows)
        out[:, c * width : (c + 1) * width] = total.astype(BF16)


def combine_body(bwd_ids, bwd_gates, fwd_ids, fwd_gates, back, routed, grad, turn):
    combine_rows(False, bwd_ids, bwd_gates, back, BWD_BACK * PACKED, grad, turn)
    combine_rows(True, fwd_ids, fwd_gates, back, FWD_BACK * PACKED, routed, turn)


def combine(routes, back):
    tokens = routes[0].shape[1]
    out = jax.ShapeDtypeStruct((tokens, back.shape[2] * CHUNKS), BF16)
    return pl.pallas_call(
        combine_body,
        out_shape=[out, out],
        scratch_shapes=[pltpu.VMEM((128, tokens), F32)],
        compiler_params=pltpu.CompilerParams(vmem_limit_bytes=60 * 2**20),
        cost_estimate=cost(800_000_000, 4_000_000),
    )(*routes, back)


def unpack_rows(packed, rows, base):
    width = packed.shape[2]
    at = iota((ROWS, SPAN), 0)
    lane = iota((ROWS, SPAN), 1)
    source, line = lane // TILE, lax.rem(lane, TILE)
    for c in range(CHUNKS):
        total = jnp.zeros((ROWS, width), F32)
        for j, _, shift in [m for m in MEETS if m[1] == c]:
            slot = line + shift
            hit = (at == source * CAP + slot) & (slot >= 0) & (slot < CAP)
            lines = slice(base + j * TILE, base + (j + 1) * TILE)
            tile = packed[:, lines, :].reshape(SPAN, width)
            total = total + dot(hit.astype(F32).astype(BF16), tile)
        rows[:, c * width : (c + 1) * width] = total.astype(BF16)


def pack_rows(rows, packed, base):
    width = packed.shape[2]
    at = iota((SPAN, ROWS), 1)
    place = iota((SPAN, ROWS), 0)
    source, line = place // TILE, lax.rem(place, TILE)
    for j in range(TILES):
        total = jnp.zeros((SPAN, width), F32)
        for _, c, shift in [m for m in MEETS if m[0] == j]:
            slot = line + shift
            hit = (at == source * CAP + slot) & (slot >= 0) & (slot < CAP)
            piece = rows[:, c * width : (c + 1) * width].astype(BF16)
            total = total + dot(hit.astype(F32).astype(BF16), piece)
        lines = slice(base + j * TILE, base + (j + 1) * TILE)
        packed[:, lines, :] = total.astype(BF16).reshape(EXPERTS, TILE, width)


def experts_body(*refs):
    got, weights = refs[0], refs[1 : 1 + 3 * SHARDS]
    back, rows, scaled, sent, bwd_total, fwd_total, held, ready = refs[1 + 3 * SHARDS :]
    copies = [
        pltpu.make_async_copy(w, held.at[n], ready.at[n]) for n, w in enumerate(weights)
    ]
    for copy in copies:
        copy.start()
    unpack_rows(got, rows, BWD * PACKED)
    unpack_rows(got, scaled, SCALED * PACKED)
    unpack_rows(got, sent, FWD * PACKED)
    for n in range(SHARDS):
        for copy in copies[3 * n : 3 * n + 3]:
            copy.wait()
        gate, up, down = held.at[3 * n], held.at[3 * n + 1], held.at[3 * n + 2]
        gate_back = dot_nt(rows[...], gate[...])
        up_back = dot_nt(rows[...], up[...])
        dact = dot_nt(scaled[...], down[...])
        sigma = 1.0 / (1.0 + jnp.exp(-gate_back))
        dgate = (dact * up_back * sigma * (1.0 + gate_back * (1.0 - sigma))).astype(BF16)
        dup = (dact * (gate_back * sigma)).astype(BF16)
        part = dot(dgate, gate[...]) + dot(dup, up[...])
        bwd_total[...] = part if n == 0 else bwd_total[...] + part

        gate_pre = dot_nt(sent[...], gate[...])
        up_pre = dot_nt(sent[...], up[...])
        act = (gate_pre / (1.0 + jnp.exp(-gate_pre)) * up_pre).astype(BF16)
        part = dot(act, down[...])
        fwd_total[...] = part if n == 0 else fwd_total[...] + part
    pack_rows(bwd_total, back, BWD_BACK * PACKED)
    pack_rows(fwd_total, back, FWD_BACK * PACKED)


def experts_of(got, weights):
    width = got.shape[2] * CHUNKS
    scratch = [pltpu.VMEM((ROWS, width), BF16)] * 3 + [
        pltpu.VMEM((ROWS, width), F32),
        pltpu.VMEM((ROWS, width), F32),
        pltpu.VMEM((len(weights),) + weights[0].shape, BF16),
        pltpu.SemaphoreType.DMA((len(weights),)),
    ]
    return pl.pallas_call(
        experts_body,
        out_shape=jax.ShapeDtypeStruct((EXPERTS, 2 * PACKED, got.shape[2]), BF16),
        in_specs=[pl.BlockSpec()] + [HBM] * len(weights),
        scratch_shapes=scratch,
        compiler_params=pltpu.CompilerParams(vmem_limit_bytes=60 * 2**20),
        cost_estimate=cost(8_000_000_000, 14_000_000),
    )(got, *weights)


def from_behind(x, axis, by):
    devices = lax.axis_size(axis)
    pairs = [(i, i + by) for i in range(devices) if 0 <= i + by < devices]
    return lax.ppermute(x, axis, pairs)


def swap(x, axis):
    return lax.ppermute(x, axis, [(0, 1), (1, 0)])


def exchange(x):
    return lax.all_to_all(x, ("plane", "pair"), split_axis=0, concat_axis=0, tiled=True)


def shards(
    fwd_act, fwd_ids, fwd_gates, bwd_input, bwd_ids, bwd_gates, bwd_grad, w_gate, w_up, w_down
):
    section_at = lax.axis_index("section")
    sections = lax.axis_size("section")
    edges = jnp.stack([section_at == 0, section_at == sections - 1]).astype(jnp.int32)
    routes = (bwd_ids[0].T, bwd_gates[0].T, fwd_ids[0].T, fwd_gates[0].T)
    own = [w_gate[0].T, w_up[0].T, w_down[0]]

    arriving = from_behind(bwd_grad[0], "section", -1)
    shifted = from_behind(fwd_act[0], "section", 1)
    across = [swap(x, "half") for x in own]
    beside = [swap(x, "core") for x in own]
    beyond = [swap(x, "core") for x in across]

    states = (bwd_input[0], bwd_grad[0], arriving, fwd_act[0], shifted)
    got = exchange(pick(edges, routes, states, [across[2]]))
    back = exchange(experts_of(got, own + beside + across + beyond))
    routed_out, input_grad = combine(routes, back)
    return (routed_out[None], input_grad[None])


def solution(mesh):
    sections, devices = mesh.devices.shape
    planes = 4
    parted = Mesh(
        mesh.devices.reshape(sections, planes, devices // planes // 4, 2, 2),
        ("section", "plane", "pair", "half", "core"),
    )
    expert = ("plane", "pair", "half", "core")
    rows = P("section", expert, None)
    columns = P("section", None, expert)
    return jax.shard_map(
        shards,
        mesh=parted,
        in_specs=(rows,) * 7 + (columns, columns, rows),
        out_specs=(rows, rows),
        check_vma=False,
    )
```

```python
import functools

import jax
import jax.numpy as jnp
from jax import lax
from jax.experimental import pallas as pl
from jax.experimental.pallas import tpu as pltpu
from jax.sharding import Mesh
from jax.sharding import PartitionSpec as P

EXPERTS = 16
SHARDS = 4
CAP = 10
TILE = 16
CHUNKS = 8
ROWS = EXPERTS * CAP
SPAN = EXPERTS * TILE
PACKED = CAP * CHUNKS
TILES = PACKED // TILE
NONE = -100.0
MARK_FLOPS = 200_000_000_000

BWD, SCALED, FWD = 0, 1, 2
BWD_BACK, FWD_BACK = 0, 1

MEETS = [
    (j, c, TILE * j - CAP * c)
    for j in range(TILES)
    for c in range(CHUNKS)
    if -TILE < TILE * j - CAP * c < CAP
]

BF16 = jnp.bfloat16
F32 = jnp.float32
NT = (((1,), (1,)), ((), ()))
HBM = pl.BlockSpec(memory_space=pltpu.HBM)
SMEM = pl.BlockSpec(memory_space=pltpu.SMEM)


def iota(shape, dim):
    return lax.broadcasted_iota(jnp.int32, shape, dim)


def dot(a, b):
    return jnp.dot(a, b, preferred_element_type=F32)


def dot_nt(a, b):
    return lax.dot_general(a, b, NT, preferred_element_type=F32)


def halves(values):
    upper = values.astype(BF16)
    return upper, (values - upper.astype(F32)).astype(BF16)


def cost(flops, size):
    return pl.CostEstimate(flops=flops, bytes_accessed=size, transcendentals=0)


def keys_by_expert(ids, gates):
    top, tokens = ids.shape
    expert = iota((EXPERTS, tokens), 0)
    chosen = jnp.zeros((EXPERTS, tokens), F32)
    gate = jnp.zeros((EXPERTS, tokens), F32)
    for k in range(top):
        hit = ids[k : k + 1, :] == expert
        chosen = chosen + hit.astype(F32)
        gate = gate + jnp.where(hit, gates[k : k + 1, :], 0.0)
    earlier = (iota((tokens, tokens), 0) < iota((tokens, tokens), 1)).astype(F32).astype(BF16)
    slot = dot(chosen.astype(BF16), earlier)
    return jnp.where(chosen > 0, slot, NONE), gate


def spread_rows(values):
    experts, tokens = values.shape
    wide = jnp.broadcast_to(values[:, None, :], (experts, TILE, tokens))
    return wide.reshape(experts * TILE, tokens)


def pick_rows(key, gate, states, out):
    key = spread_rows(key)
    row = lax.rem(iota(key.shape, 0), TILE).astype(F32)
    parts = [1.0]
    if gate is not None:
        parts = [h.astype(F32) for h in halves(spread_rows(gate))]
    width = states.shape[1] // CHUNKS
    for j in range(TILES):
        total = jnp.zeros((SPAN, width), F32)
        for _, c, shift in [m for m in MEETS if m[0] == j]:
            hit = key == row + float(shift)
            piece = states[:, c * width : (c + 1) * width]
            for part in parts:
                total = total + dot(jnp.where(hit, part, 0.0).astype(BF16), piece)
        out[:, j * TILE : (j + 1) * TILE, :] = total.astype(BF16).reshape(EXPERTS, TILE, width)


def pick_body(edges, bwd_ids, bwd_gates, fwd_ids, fwd_gates, *refs):
    bwd_input, bwd_grad, arriving, fwd_act, shifted = refs[:5]
    out, states, packed, read, written = refs[-5:]

    def fetch(source, n):
        return pltpu.make_async_copy(source, states.at[n], read.at[n])

    def fetch_one_of(edge, own, moved, n):
        @pl.when(edge == 1)
        def _():
            fetch(own, n).start()

        @pl.when(edge != 1)
        def _():
            fetch(moved, n).start()

    def store(n):
        lines = pl.ds(n * PACKED, PACKED)
        return pltpu.make_async_copy(packed.at[n], out.at[:, lines, :], written.at[n])

    fetch(bwd_input, BWD).start()
    fetch_one_of(edges[1], bwd_grad, arriving, SCALED)
    fetch_one_of(edges[0], fwd_act, shifted, FWD)
    bwd_key, bwd_gate = keys_by_expert(bwd_ids, bwd_gates)
    fwd_key, _ = keys_by_expert(fwd_ids, fwd_gates)
    for n, key, gate in (
        (BWD, bwd_key, None),
        (SCALED, bwd_key, bwd_gate),
        (FWD, fwd_key, None),
    ):
        fetch(bwd_input, n).wait()
        pick_rows(key, gate, states.at[n], packed.at[n])
        store(n).start()
    for n in (BWD, SCALED, FWD):
        store(n).wait()


def pick(edges, routes, states):
    tokens, width = states[0].shape
    out = (EXPERTS, 3 * PACKED, width // CHUNKS)
    return pl.pallas_call(
        pick_body,
        out_shape=jax.ShapeDtypeStruct(out, BF16),
        in_specs=[SMEM] + [pl.BlockSpec()] * 4 + [HBM] * len(states),
        out_specs=HBM,
        scratch_shapes=[
            pltpu.VMEM((3, tokens, width), BF16),
            pltpu.VMEM((3, EXPERTS, PACKED, width // CHUNKS), BF16),
            pltpu.SemaphoreType.DMA((3,)),
            pltpu.SemaphoreType.DMA((3,)),
        ],
        compiler_params=pltpu.CompilerParams(vmem_limit_bytes=60 * 2**20),
        cost_estimate=cost(1_600_000_000, 5_000_000),
    )(edges, *routes, *states)


def combine_rows(weighted, ids, gates, back, base, out, turn):
    tokens = out.shape[0]
    key, gate = keys_by_expert(ids, gates)
    turn[:EXPERTS] = key
    turn[EXPERTS : 2 * EXPERTS] = gate
    turn[2 * EXPERTS :] = jnp.zeros((128 - 2 * EXPERTS, tokens), F32)
    turned = turn[...].T
    column, source = iota((128, SPAN), 0), iota((128, SPAN), 1) // TILE
    key = dot(turned.astype(BF16), (column == source).astype(F32).astype(BF16))
    widen = (column == source + EXPERTS).astype(F32).astype(BF16)
    row = lax.rem(iota(key.shape, 1), TILE).astype(F32)
    parts = [1.0]
    if weighted:
        parts = [dot(h, widen) for h in halves(turned)]
    width = out.shape[1] // CHUNKS
    for c in range(CHUNKS):
        total = jnp.zeros((tokens, width), F32)
        for j, _, shift in [m for m in MEETS if m[1] == c]:
            hit = key == row + float(shift)
            lines = slice(base + j * TILE, base + (j + 1) * TILE)
            rows = back[:, lines, :].reshape(SPAN, width)
            for part in parts:
                total = total + dot(jnp.where(hit, part, 0.0).astype(BF16), rows)
        out[:, c * width : (c + 1) * width] = total.astype(BF16)


def combine_body(bwd_ids, bwd_gates, fwd_ids, fwd_gates, back, routed, grad, turn):
    combine_rows(False, bwd_ids, bwd_gates, back, BWD_BACK * PACKED, grad, turn)
    combine_rows(True, fwd_ids, fwd_gates, back, FWD_BACK * PACKED, routed, turn)


def combine(routes, back):
    tokens = routes[0].shape[1]
    out = jax.ShapeDtypeStruct((tokens, back.shape[2] * CHUNKS), BF16)
    return pl.pallas_call(
        combine_body,
        out_shape=[out, out],
        scratch_shapes=[pltpu.VMEM((128, tokens), F32)],
        compiler_params=pltpu.CompilerParams(vmem_limit_bytes=60 * 2**20),
        cost_estimate=cost(800_000_000, 4_000_000),
    )(*routes, back)


def unpack_rows(packed, rows, base):
    width = packed.shape[2]
    at = iota((ROWS, SPAN), 0)
    lane = iota((ROWS, SPAN), 1)
    source, line = lane // TILE, lax.rem(lane, TILE)
    for c in range(CHUNKS):
        total = jnp.zeros((ROWS, width), F32)
        for j, _, shift in [m for m in MEETS if m[1] == c]:
            slot = line + shift
            hit = (at == source * CAP + slot) & (slot >= 0) & (slot < CAP)
            lines = slice(base + j * TILE, base + (j + 1) * TILE)
            tile = packed[:, lines, :].reshape(SPAN, width)
            total = total + dot(hit.astype(F32).astype(BF16), tile)
        rows[:, c * width : (c + 1) * width] = total.astype(BF16)


def pack_rows(rows, packed, base):
    width = packed.shape[2]
    at = iota((SPAN, ROWS), 1)
    place = iota((SPAN, ROWS), 0)
    source, line = place // TILE, lax.rem(place, TILE)
    for j in range(TILES):
        total = jnp.zeros((SPAN, width), F32)
        for _, c, shift in [m for m in MEETS if m[0] == j]:
            slot = line + shift
            hit = (at == source * CAP + slot) & (slot >= 0) & (slot < CAP)
            piece = rows[:, c * width : (c + 1) * width].astype(BF16)
            total = total + dot(hit.astype(F32).astype(BF16), piece)
        lines = slice(base + j * TILE, base + (j + 1) * TILE)
        packed[:, lines, :] = total.astype(BF16).reshape(EXPERTS, TILE, width)


def experts_body(*refs):
    got, weights, beside = refs[0], list(refs[1 : 3 * SHARDS - 2]), refs[3 * SHARDS - 2]
    weights += [beside.at[i] for i in range(3)]
    back, rows, scaled, sent, bwd_total, fwd_total, held, ready = refs[-8:]
    copies = [
        pltpu.make_async_copy(w, held.at[n], ready.at[n]) for n, w in enumerate(weights)
    ]
    for copy in copies:
        copy.start()
    unpack_rows(got, rows, BWD * PACKED)
    unpack_rows(got, scaled, SCALED * PACKED)
    unpack_rows(got, sent, FWD * PACKED)
    for n in range(SHARDS):
        for copy in copies[3 * n : 3 * n + 3]:
            copy.wait()
        gate, up, down = held.at[3 * n], held.at[3 * n + 1], held.at[3 * n + 2]
        gate_back = dot_nt(rows[...], gate[...])
        up_back = dot_nt(rows[...], up[...])
        dact = dot_nt(scaled[...], down[...])
        sigma = 1.0 / (1.0 + jnp.exp(-gate_back))
        dgate = (dact * up_back * sigma * (1.0 + gate_back * (1.0 - sigma))).astype(BF16)
        dup = (dact * (gate_back * sigma)).astype(BF16)
        part = dot(dgate, gate[...]) + dot(dup, up[...])
        bwd_total[...] = part if n == 0 else bwd_total[...] + part

        gate_pre = dot_nt(sent[...], gate[...])
        up_pre = dot_nt(sent[...], up[...])
        act = (gate_pre / (1.0 + jnp.exp(-gate_pre)) * up_pre).astype(BF16)
        part = dot(act, down[...])
        fwd_total[...] = part if n == 0 else fwd_total[...] + part
    pack_rows(bwd_total, back, BWD_BACK * PACKED)
    pack_rows(fwd_total, back, FWD_BACK * PACKED)


def experts_of(got, weights, beside, after):
    width = got.shape[2] * CHUNKS
    scratch = [pltpu.VMEM((ROWS, width), BF16)] * 3 + [
        pltpu.VMEM((ROWS, width), F32),
        pltpu.VMEM((ROWS, width), F32),
        pltpu.VMEM((3 * SHARDS,) + weights[0].shape, BF16),
        pltpu.SemaphoreType.DMA((3 * SHARDS,)),
    ]
    return pl.pallas_call(
        experts_body,
        out_shape=jax.ShapeDtypeStruct((EXPERTS, 2 * PACKED, got.shape[2]), BF16),
        in_specs=[pl.BlockSpec()] + [HBM] * (len(weights) + 2),
        scratch_shapes=scratch,
        compiler_params=pltpu.CompilerParams(vmem_limit_bytes=60 * 2**20),
        cost_estimate=cost(8_000_000_000, 14_000_000),
    )(got, *weights, beside, after)


def stack_body(*refs):
    arrays, out, done = refs[:3], refs[-2], refs[-1]
    copies = [pltpu.make_async_copy(w, out.at[i], done.at[i]) for i, w in enumerate(arrays)]
    for copy in copies:
        copy.start()
    for copy in copies:
        copy.wait()


def stack(arrays, after):
    n = len(arrays)
    return pl.pallas_call(
        stack_body,
        out_shape=jax.ShapeDtypeStruct((n,) + arrays[0].shape, BF16),
        in_specs=[HBM] * (n + 1),
        out_specs=HBM,
        scratch_shapes=[pltpu.SemaphoreType.DMA((n,))],
        cost_estimate=cost(0, 5_000_000),
    )(*arrays, after)


def mark_body(ids, out):
    out[...] = jnp.zeros_like(out) + ids[0, 0]


def mark(ids):
    return pl.pallas_call(
        mark_body,
        out_shape=jax.ShapeDtypeStruct((8, 128), jnp.int32),
        in_specs=[SMEM],
        cost_estimate=cost(MARK_FLOPS, 0),
    )(ids)


def from_behind(x, axis, by):
    devices = lax.axis_size(axis)
    pairs = [(i, i + by) for i in range(devices) if 0 <= i + by < devices]
    return lax.ppermute(x, axis, pairs)


def swap(x, axis):
    return lax.ppermute(x, axis, [(0, 1), (1, 0)])


def exchange(x):
    return lax.all_to_all(x, ("plane", "pair"), split_axis=0, concat_axis=0, tiled=True)


def shards(
    fwd_act, fwd_ids, fwd_gates, bwd_input, bwd_ids, bwd_gates, bwd_grad, w_gate, w_up, w_down
):
    section_at = lax.axis_index("section")
    sections = lax.axis_size("section")
    edges = jnp.stack([section_at == 0, section_at == sections - 1]).astype(jnp.int32)
    routes = (bwd_ids[0].T, bwd_gates[0].T, fwd_ids[0].T, fwd_gates[0].T)
    own = [w_gate[0].T, w_up[0].T, w_down[0]]

    arriving = from_behind(bwd_grad[0], "section", -1)
    shifted = from_behind(fwd_act[0], "section", 1)
    across = [swap(x, "half") for x in own]
    beyond = [swap(x, "core") for x in across]

    states = (bwd_input[0], bwd_grad[0], arriving, fwd_act[0], shifted)
    sent = pick(edges, routes, states)
    beside = swap(stack(own, sent), "core")
    got = exchange(sent)
    back = exchange(experts_of(got, own + across + beyond, beside, mark(routes[0])))
    routed_out, input_grad = combine(routes, back)
    return (routed_out[None], input_grad[None])


def solution(mesh):
    sections, devices = mesh.devices.shape
    planes = 4
    parted = Mesh(
        mesh.devices.reshape(sections, planes, devices // planes // 4, 2, 2),
        ("section", "plane", "pair", "half", "core"),
    )
    expert = ("plane", "pair", "half", "core")
    rows = P("section", expert, None)
    columns = P("section", None, expert)
    return jax.shard_map(
        shards,
        mesh=parted,
        in_specs=(rows,) * 7 + (columns, columns, rows),
        out_specs=(rows, rows),
        check_vma=False,
    )
```

```python
import functools

import jax
import jax.numpy as jnp
from jax import lax
from jax.experimental import pallas as pl
from jax.experimental.pallas import tpu as pltpu
from jax.sharding import Mesh
from jax.sharding import PartitionSpec as P

EXPERTS = 16
SHARDS = 4
CAP = 10
TILE = 16
CHUNKS = 8
ROWS = EXPERTS * CAP
SPAN = EXPERTS * TILE
PACKED = CAP * CHUNKS
TILES = PACKED // TILE
NONE = -100.0
MARK_FLOPS = 200_000_000_000

BWD, SCALED, FWD = 0, 1, 2
BWD_BACK, FWD_BACK = 0, 1

MEETS = [
    (j, c, TILE * j - CAP * c)
    for j in range(TILES)
    for c in range(CHUNKS)
    if -TILE < TILE * j - CAP * c < CAP
]

BF16 = jnp.bfloat16
F32 = jnp.float32
NT = (((1,), (1,)), ((), ()))
HBM = pl.BlockSpec(memory_space=pltpu.HBM)
SMEM = pl.BlockSpec(memory_space=pltpu.SMEM)


def iota(shape, dim):
    return lax.broadcasted_iota(jnp.int32, shape, dim)


def dot(a, b):
    return jnp.dot(a, b, preferred_element_type=F32)


def dot_nt(a, b):
    return lax.dot_general(a, b, NT, preferred_element_type=F32)


def halves(values):
    upper = values.astype(BF16)
    return upper, (values - upper.astype(F32)).astype(BF16)


def cost(flops, size):
    return pl.CostEstimate(flops=flops, bytes_accessed=size, transcendentals=0)


def keys_by_expert(ids, gates):
    top, tokens = ids.shape
    expert = iota((EXPERTS, tokens), 0)
    chosen = jnp.zeros((EXPERTS, tokens), F32)
    gate = jnp.zeros((EXPERTS, tokens), F32)
    for k in range(top):
        hit = ids[k : k + 1, :] == expert
        chosen = chosen + hit.astype(F32)
        gate = gate + jnp.where(hit, gates[k : k + 1, :], 0.0)
    earlier = (iota((tokens, tokens), 0) < iota((tokens, tokens), 1)).astype(F32).astype(BF16)
    slot = dot(chosen.astype(BF16), earlier)
    return jnp.where(chosen > 0, slot, NONE), gate


def spread_rows(values):
    experts, tokens = values.shape
    wide = jnp.broadcast_to(values[:, None, :], (experts, TILE, tokens))
    return wide.reshape(experts * TILE, tokens)


def pick_rows(key, gate, states, out):
    key = spread_rows(key)
    row = lax.rem(iota(key.shape, 0), TILE).astype(F32)
    parts = [1.0]
    if gate is not None:
        parts = [h.astype(F32) for h in halves(spread_rows(gate))]
    width = states.shape[1] // CHUNKS
    for j in range(TILES):
        total = jnp.zeros((SPAN, width), F32)
        for _, c, shift in [m for m in MEETS if m[0] == j]:
            hit = key == row + float(shift)
            piece = states[:, c * width : (c + 1) * width]
            for part in parts:
                total = total + dot(jnp.where(hit, part, 0.0).astype(BF16), piece)
        out[:, j * TILE : (j + 1) * TILE, :] = total.astype(BF16).reshape(EXPERTS, TILE, width)


def pick_body(edges, bwd_ids, bwd_gates, fwd_ids, fwd_gates, *refs):
    bwd_input, bwd_grad, arriving, fwd_act, shifted = refs[:5]
    out, states, packed, read, written = refs[-5:]

    def fetch(source, n):
        return pltpu.make_async_copy(source, states.at[n], read.at[n])

    def fetch_one_of(edge, own, moved, n):
        @pl.when(edge == 1)
        def _():
            fetch(own, n).start()

        @pl.when(edge != 1)
        def _():
            fetch(moved, n).start()

    def store(n):
        lines = pl.ds(n * PACKED, PACKED)
        return pltpu.make_async_copy(packed.at[n], out.at[:, lines, :], written.at[n])

    fetch(bwd_input, BWD).start()
    fetch_one_of(edges[1], bwd_grad, arriving, SCALED)
    fetch_one_of(edges[0], fwd_act, shifted, FWD)
    bwd_key, bwd_gate = keys_by_expert(bwd_ids, bwd_gates)
    fwd_key, _ = keys_by_expert(fwd_ids, fwd_gates)
    for n, key, gate in (
        (BWD, bwd_key, None),
        (SCALED, bwd_key, bwd_gate),
        (FWD, fwd_key, None),
    ):
        fetch(bwd_input, n).wait()
        pick_rows(key, gate, states.at[n], packed.at[n])
        store(n).start()
    for n in (BWD, SCALED, FWD):
        store(n).wait()


def pick(edges, routes, states):
    tokens, width = states[0].shape
    out = (EXPERTS, 3 * PACKED, width // CHUNKS)
    return pl.pallas_call(
        pick_body,
        out_shape=jax.ShapeDtypeStruct(out, BF16),
        in_specs=[SMEM] + [pl.BlockSpec()] * 4 + [HBM] * len(states),
        out_specs=HBM,
        scratch_shapes=[
            pltpu.VMEM((3, tokens, width), BF16),
            pltpu.VMEM((3, EXPERTS, PACKED, width // CHUNKS), BF16),
            pltpu.SemaphoreType.DMA((3,)),
            pltpu.SemaphoreType.DMA((3,)),
        ],
        compiler_params=pltpu.CompilerParams(vmem_limit_bytes=60 * 2**20),
        cost_estimate=cost(1_600_000_000, 5_000_000),
    )(edges, *routes, *states)


def combine_rows(weighted, ids, gates, back, base, out, turn):
    tokens = out.shape[0]
    key, gate = keys_by_expert(ids, gates)
    turn[:EXPERTS] = key
    turn[EXPERTS : 2 * EXPERTS] = gate
    turn[2 * EXPERTS :] = jnp.zeros((128 - 2 * EXPERTS, tokens), F32)
    turned = turn[...].T
    column, source = iota((128, SPAN), 0), iota((128, SPAN), 1) // TILE
    key = dot(turned.astype(BF16), (column == source).astype(F32).astype(BF16))
    widen = (column == source + EXPERTS).astype(F32).astype(BF16)
    row = lax.rem(iota(key.shape, 1), TILE).astype(F32)
    parts = [1.0]
    if weighted:
        parts = [dot(h, widen) for h in halves(turned)]
    width = out.shape[1] // CHUNKS
    for c in range(CHUNKS):
        total = jnp.zeros((tokens, width), F32)
        for j, _, shift in [m for m in MEETS if m[1] == c]:
            hit = key == row + float(shift)
            lines = slice(base + j * TILE, base + (j + 1) * TILE)
            rows = back[:, lines, :].reshape(SPAN, width)
            for part in parts:
                total = total + dot(jnp.where(hit, part, 0.0).astype(BF16), rows)
        out[:, c * width : (c + 1) * width] = total.astype(BF16)


def combine_body(bwd_ids, bwd_gates, fwd_ids, fwd_gates, back, routed, grad, turn):
    combine_rows(False, bwd_ids, bwd_gates, back, BWD_BACK * PACKED, grad, turn)
    combine_rows(True, fwd_ids, fwd_gates, back, FWD_BACK * PACKED, routed, turn)


def combine(routes, back):
    tokens = routes[0].shape[1]
    out = jax.ShapeDtypeStruct((tokens, back.shape[2] * CHUNKS), BF16)
    return pl.pallas_call(
        combine_body,
        out_shape=[out, out],
        scratch_shapes=[pltpu.VMEM((128, tokens), F32)],
        compiler_params=pltpu.CompilerParams(vmem_limit_bytes=60 * 2**20),
        cost_estimate=cost(800_000_000, 4_000_000),
    )(*routes, back)


def unpack_rows(packed, rows, base):
    width = packed.shape[2]
    at = iota((ROWS, SPAN), 0)
    lane = iota((ROWS, SPAN), 1)
    source, line = lane // TILE, lax.rem(lane, TILE)
    for c in range(CHUNKS):
        total = jnp.zeros((ROWS, width), F32)
        for j, _, shift in [m for m in MEETS if m[1] == c]:
            slot = line + shift
            hit = (at == source * CAP + slot) & (slot >= 0) & (slot < CAP)
            lines = slice(base + j * TILE, base + (j + 1) * TILE)
            tile = packed[:, lines, :].reshape(SPAN, width)
            total = total + dot(hit.astype(F32).astype(BF16), tile)
        rows[:, c * width : (c + 1) * width] = total.astype(BF16)


def pack_rows(rows, packed, base):
    width = packed.shape[2]
    at = iota((SPAN, ROWS), 1)
    place = iota((SPAN, ROWS), 0)
    source, line = place // TILE, lax.rem(place, TILE)
    for j in range(TILES):
        total = jnp.zeros((SPAN, width), F32)
        for _, c, shift in [m for m in MEETS if m[0] == j]:
            slot = line + shift
            hit = (at == source * CAP + slot) & (slot >= 0) & (slot < CAP)
            piece = rows[:, c * width : (c + 1) * width]
            total = total + dot(hit.astype(F32).astype(BF16), piece)
        lines = slice(base + j * TILE, base + (j + 1) * TILE)
        packed[:, lines, :] = total.astype(BF16).reshape(EXPERTS, TILE, width)


def experts_body(*refs):
    got, weights, beside = refs[0], list(refs[1 : 3 * SHARDS - 2]), refs[3 * SHARDS - 2]
    weights += [beside.at[i] for i in range(3)]
    back, rows, scaled, bwd_total, fwd_total, held, ready = refs[-7:]
    hidden = weights[0].shape[0]
    copies = []
    for n, w in enumerate(weights):
        units = pl.ds(n // 3 * hidden, hidden)
        copies.append(pltpu.make_async_copy(w, held.at[n % 3, units], ready.at[n]))
    for copy in copies:
        copy.start()
    unpack_rows(got, rows.at[:ROWS], BWD * PACKED)
    unpack_rows(got, rows.at[ROWS:], FWD * PACKED)
    unpack_rows(got, scaled, SCALED * PACKED)
    for copy in copies:
        copy.wait()
    gate, up, down = held.at[0], held.at[1], held.at[2]
    gates = dot_nt(rows[...], gate[...])
    ups = dot_nt(rows[...], up[...])
    gate_back, gate_pre = gates[:ROWS], gates[ROWS:]
    up_back, up_pre = ups[:ROWS], ups[ROWS:]
    act = (gate_pre / (1.0 + jnp.exp(-gate_pre)) * up_pre).astype(BF16)
    dact = dot_nt(scaled[...], down[...])
    sigma = 1.0 / (1.0 + jnp.exp(-gate_back))
    dgate = (dact * up_back * sigma * (1.0 + gate_back * (1.0 - sigma))).astype(BF16)
    dup = (dact * (gate_back * sigma)).astype(BF16)
    bwd_total[...] = (dot(dgate, gate[...]) + dot(dup, up[...])).astype(BF16)
    fwd_total[...] = dot(act, down[...]).astype(BF16)
    pack_rows(bwd_total, back, BWD_BACK * PACKED)
    pack_rows(fwd_total, back, FWD_BACK * PACKED)


def experts_of(got, weights, beside, after):
    width = got.shape[2] * CHUNKS
    scratch = [
        pltpu.VMEM((2 * ROWS, width), BF16),
        pltpu.VMEM((ROWS, width), BF16),
        pltpu.VMEM((ROWS, width), BF16),
        pltpu.VMEM((ROWS, width), BF16),
        pltpu.VMEM((3, SHARDS * weights[0].shape[0], width), BF16),
        pltpu.SemaphoreType.DMA((3 * SHARDS,)),
    ]
    return pl.pallas_call(
        experts_body,
        out_shape=jax.ShapeDtypeStruct((EXPERTS, 2 * PACKED, got.shape[2]), BF16),
        in_specs=[pl.BlockSpec()] + [HBM] * (len(weights) + 2),
        scratch_shapes=scratch,
        compiler_params=pltpu.CompilerParams(vmem_limit_bytes=60 * 2**20),
        cost_estimate=cost(8_000_000_000, 14_000_000),
    )(got, *weights, beside, after)


def stack_body(gate, up, down, after, out):
    del after
    out[0] = gate[...]
    out[1] = up[...]
    out[2] = down[...]


def stack(arrays, after):
    return pl.pallas_call(
        stack_body,
        out_shape=jax.ShapeDtypeStruct((3,) + arrays[0].shape, BF16),
        in_specs=[pl.BlockSpec()] * 3 + [HBM],
        compiler_params=pltpu.CompilerParams(vmem_limit_bytes=60 * 2**20),
        cost_estimate=cost(0, 5_000_000),
    )(*arrays, after)


def mark_body(ids, out):
    out[...] = jnp.zeros_like(out) + ids[0, 0]


def mark(ids):
    return pl.pallas_call(
        mark_body,
        out_shape=jax.ShapeDtypeStruct((8, 128), jnp.int32),
        in_specs=[SMEM],
        cost_estimate=cost(MARK_FLOPS, 0),
    )(ids)


def from_behind(x, axis, by):
    devices = lax.axis_size(axis)
    pairs = [(i, i + by) for i in range(devices) if 0 <= i + by < devices]
    return lax.ppermute(x, axis, pairs)


def swap(x, axis):
    return lax.ppermute(x, axis, [(0, 1), (1, 0)])


def exchange(x):
    return lax.all_to_all(x, ("plane", "pair"), split_axis=0, concat_axis=0, tiled=True)


def shards(
    fwd_act, fwd_ids, fwd_gates, bwd_input, bwd_ids, bwd_gates, bwd_grad, w_gate, w_up, w_down
):
    section_at = lax.axis_index("section")
    sections = lax.axis_size("section")
    edges = jnp.stack([section_at == 0, section_at == sections - 1]).astype(jnp.int32)
    routes = (bwd_ids[0].T, bwd_gates[0].T, fwd_ids[0].T, fwd_gates[0].T)
    own = [w_gate[0].T, w_up[0].T, w_down[0]]

    arriving = from_behind(bwd_grad[0], "section", -1)
    shifted = from_behind(fwd_act[0], "section", 1)
    across = [swap(x, "half") for x in own]
    beyond = [swap(x, "core") for x in across]

    states = (bwd_input[0], bwd_grad[0], arriving, fwd_act[0], shifted)
    sent = pick(edges, routes, states)
    beside = swap(stack(own, sent), "core")
    got = exchange(sent)
    back = exchange(experts_of(got, own + across + beyond, beside, mark(routes[0])))
    routed_out, input_grad = combine(routes, back)
    return (routed_out[None], input_grad[None])


def solution(mesh):
    sections, devices = mesh.devices.shape
    planes = 4
    parted = Mesh(
        mesh.devices.reshape(sections, planes, devices // planes // 4, 2, 2),
        ("section", "plane", "pair", "half", "core"),
    )
    expert = ("plane", "pair", "half", "core")
    rows = P("section", expert, None)
    columns = P("section", None, expert)
    return jax.shard_map(
        shards,
        mesh=parted,
        in_specs=(rows,) * 7 + (columns, columns, rows),
        out_specs=(rows, rows),
        check_vma=False,
    )
```

```python
import functools

import jax
import jax.numpy as jnp
from jax import lax
from jax.experimental import pallas as pl
from jax.experimental.pallas import tpu as pltpu
from jax.sharding import Mesh
from jax.sharding import PartitionSpec as P

EXPERTS = 16
SHARDS = 4
CAP = 10
TILE = 16
CHUNKS = 8
ROWS = EXPERTS * CAP
SPAN = EXPERTS * TILE
PACKED = CAP * CHUNKS
TILES = PACKED // TILE
NONE = -100.0
MARK_FLOPS = 200_000_000_000

BWD, SCALED, FWD = 0, 1, 2
BWD_BACK, FWD_BACK = 0, 1

MEETS = [
    (j, c, TILE * j - CAP * c)
    for j in range(TILES)
    for c in range(CHUNKS)
    if -TILE < TILE * j - CAP * c < CAP
]

BF16 = jnp.bfloat16
F32 = jnp.float32
NT = (((1,), (1,)), ((), ()))
HBM = pl.BlockSpec(memory_space=pltpu.HBM)
SMEM = pl.BlockSpec(memory_space=pltpu.SMEM)


def iota(shape, dim):
    return lax.broadcasted_iota(jnp.int32, shape, dim)


def dot(a, b):
    return jnp.dot(a, b, preferred_element_type=F32)


def dot_nt(a, b):
    return lax.dot_general(a, b, NT, preferred_element_type=F32)


def one_where(place, shift):
    return jnp.where(place == float(shift), 1.0, 0.0).astype(BF16)


def halves(values):
    upper = values.astype(BF16)
    return upper, (values - upper.astype(F32)).astype(BF16)


def cost(flops, size):
    return pl.CostEstimate(flops=flops, bytes_accessed=size, transcendentals=0)


def keys_by_expert(ids, gates):
    top, tokens = ids.shape
    expert = iota((EXPERTS, tokens), 0)
    chosen = jnp.zeros((EXPERTS, tokens), F32)
    gate = jnp.zeros((EXPERTS, tokens), F32)
    for k in range(top):
        hit = ids[k : k + 1, :] == expert
        chosen = chosen + hit.astype(F32)
        gate = gate + jnp.where(hit, gates[k : k + 1, :], 0.0)
    earlier = (iota((tokens, tokens), 0) < iota((tokens, tokens), 1)).astype(F32).astype(BF16)
    slot = dot(chosen.astype(BF16), earlier)
    return jnp.where(chosen > 0, slot, NONE), gate


def spread_rows(values):
    experts, tokens = values.shape
    wide = jnp.broadcast_to(values[:, None, :], (experts, TILE, tokens))
    return wide.reshape(experts * TILE, tokens)


def pick_rows(key, gate, states, out):
    key = spread_rows(key)
    place = key - lax.rem(iota(key.shape, 0), TILE).astype(F32)
    parts = [1.0]
    if gate is not None:
        parts = [h.astype(F32) for h in halves(spread_rows(gate))]
    width = states.shape[1] // CHUNKS
    for j in range(TILES):
        total = jnp.zeros((SPAN, width), F32)
        for _, c, shift in [m for m in MEETS if m[0] == j]:
            hit = place == float(shift)
            piece = states[:, c * width : (c + 1) * width]
            for part in parts:
                total = total + dot(jnp.where(hit, part, 0.0).astype(BF16), piece)
        out[:, j * TILE : (j + 1) * TILE, :] = total.astype(BF16).reshape(EXPERTS, TILE, width)


def pick_body(edges, bwd_ids, bwd_gates, fwd_ids, fwd_gates, *refs):
    bwd_input, bwd_grad, arriving, fwd_act, shifted = refs[:5]
    out, states, packed, read, written = refs[-5:]

    def fetch(source, n):
        return pltpu.make_async_copy(source, states.at[n], read.at[n])

    def fetch_one_of(edge, own, moved, n):
        @pl.when(edge == 1)
        def _():
            fetch(own, n).start()

        @pl.when(edge != 1)
        def _():
            fetch(moved, n).start()

    def store(n):
        lines = pl.ds(n * PACKED, PACKED)
        return pltpu.make_async_copy(packed.at[n], out.at[:, lines, :], written.at[n])

    fetch(bwd_input, BWD).start()
    fetch_one_of(edges[1], bwd_grad, arriving, SCALED)
    fetch_one_of(edges[0], fwd_act, shifted, FWD)
    bwd_key, bwd_gate = keys_by_expert(bwd_ids, bwd_gates)
    fwd_key, _ = keys_by_expert(fwd_ids, fwd_gates)
    for n, key, gate in (
        (BWD, bwd_key, None),
        (SCALED, bwd_key, bwd_gate),
        (FWD, fwd_key, None),
    ):
        fetch(bwd_input, n).wait()
        pick_rows(key, gate, states.at[n], packed.at[n])
        store(n).start()
    for n in (BWD, SCALED, FWD):
        store(n).wait()


def pick(edges, routes, states):
    tokens, width = states[0].shape
    out = (EXPERTS, 3 * PACKED, width // CHUNKS)
    return pl.pallas_call(
        pick_body,
        out_shape=jax.ShapeDtypeStruct(out, BF16),
        in_specs=[SMEM] + [pl.BlockSpec()] * 4 + [HBM] * len(states),
        out_specs=HBM,
        scratch_shapes=[
            pltpu.VMEM((3, tokens, width), BF16),
            pltpu.VMEM((3, EXPERTS, PACKED, width // CHUNKS), BF16),
            pltpu.SemaphoreType.DMA((3,)),
            pltpu.SemaphoreType.DMA((3,)),
        ],
        compiler_params=pltpu.CompilerParams(vmem_limit_bytes=60 * 2**20),
        cost_estimate=cost(1_600_000_000, 5_000_000),
    )(edges, *routes, *states)


def combine_rows(weighted, ids, gates, back, base, out, turn):
    tokens = out.shape[0]
    key, gate = keys_by_expert(ids, gates)
    turn[:EXPERTS] = key
    turn[EXPERTS : 2 * EXPERTS] = gate
    turn[2 * EXPERTS :] = jnp.zeros((128 - 2 * EXPERTS, tokens), F32)
    turned = turn[...].T
    column, source = iota((128, SPAN), 0), iota((128, SPAN), 1) // TILE
    key = dot(turned.astype(BF16), (column == source).astype(F32).astype(BF16))
    widen = (column == source + EXPERTS).astype(F32).astype(BF16)
    place = key - lax.rem(iota(key.shape, 1), TILE).astype(F32)
    parts = [1.0]
    if weighted:
        parts = [dot(h, widen) for h in halves(turned)]
    width = out.shape[1] // CHUNKS
    for c in range(CHUNKS):
        total = jnp.zeros((tokens, width), F32)
        for j, _, shift in [m for m in MEETS if m[1] == c]:
            hit = place == float(shift)
            lines = slice(base + j * TILE, base + (j + 1) * TILE)
            rows = back[:, lines, :].reshape(SPAN, width)
            for part in parts:
                total = total + dot(jnp.where(hit, part, 0.0).astype(BF16), rows)
        out[:, c * width : (c + 1) * width] = total.astype(BF16)


def combine_body(bwd_ids, bwd_gates, fwd_ids, fwd_gates, back, routed, grad, turn):
    combine_rows(False, bwd_ids, bwd_gates, back, BWD_BACK * PACKED, grad, turn)
    combine_rows(True, fwd_ids, fwd_gates, back, FWD_BACK * PACKED, routed, turn)


def combine(routes, back):
    tokens = routes[0].shape[1]
    out = jax.ShapeDtypeStruct((tokens, back.shape[2] * CHUNKS), BF16)
    return pl.pallas_call(
        combine_body,
        out_shape=[out, out],
        scratch_shapes=[pltpu.VMEM((128, tokens), F32)],
        compiler_params=pltpu.CompilerParams(vmem_limit_bytes=60 * 2**20),
        cost_estimate=cost(800_000_000, 4_000_000),
    )(*routes, back)


def places(source, line, at):
    slot = at - source * CAP
    return jnp.where((slot >= 0) & (slot < CAP), slot - line, int(NONE)).astype(F32)


def unpack_rows(packed, arrays):
    width = packed.shape[2]
    lane = iota((ROWS, SPAN), 1)
    place = places(lane // TILE, lax.rem(lane, TILE), iota((ROWS, SPAN), 0))
    for c in range(CHUNKS):
        totals = {n: jnp.zeros((ROWS, width), F32) for n in arrays}
        for j, _, shift in [m for m in MEETS if m[1] == c]:
            hit = one_where(place, shift)
            for n in arrays:
                lines = slice(n * PACKED + j * TILE, n * PACKED + (j + 1) * TILE)
                totals[n] = totals[n] + dot(hit, packed[:, lines, :].reshape(SPAN, width))
        for n, rows in arrays.items():
            rows[:, c * width : (c + 1) * width] = totals[n].astype(BF16)


def pack_rows(arrays, packed):
    width = packed.shape[2]
    line = iota((SPAN, ROWS), 0)
    place = places(line // TILE, lax.rem(line, TILE), iota((SPAN, ROWS), 1))
    for j in range(TILES):
        totals = {n: jnp.zeros((SPAN, width), F32) for n in arrays}
        for _, c, shift in [m for m in MEETS if m[0] == j]:
            hit = one_where(place, shift)
            for n, rows in arrays.items():
                totals[n] = totals[n] + dot(hit, rows[:, c * width : (c + 1) * width])
        for n in arrays:
            lines = slice(n * PACKED + j * TILE, n * PACKED + (j + 1) * TILE)
            packed[:, lines, :] = totals[n].astype(BF16).reshape(EXPERTS, TILE, width)


def experts_body(*refs):
    got, weights = refs[0], refs[1 : 1 + SHARDS]
    back, rows, scaled, bwd_total, fwd_total, held, ready = refs[-7:]
    hidden = weights[0].shape[1]
    copies = [
        pltpu.make_async_copy(w, held.at[:, pl.ds(n * hidden, hidden)], ready.at[n])
        for n, w in enumerate(weights)
    ]
    for copy in copies:
        copy.start()
    unpack_rows(got, {BWD: rows.at[:ROWS], FWD: rows.at[ROWS:], SCALED: scaled})
    for copy in copies:
        copy.wait()
    gate, up, down = held.at[0], held.at[1], held.at[2]
    gates = dot_nt(rows[...], gate[...])
    ups = dot_nt(rows[...], up[...])
    gate_back, gate_pre = gates[:ROWS], gates[ROWS:]
    up_back, up_pre = ups[:ROWS], ups[ROWS:]
    act = (gate_pre / (1.0 + jnp.exp(-gate_pre)) * up_pre).astype(BF16)
    dact = dot_nt(scaled[...], down[...])
    sigma = 1.0 / (1.0 + jnp.exp(-gate_back))
    dgate = (dact * up_back * sigma * (1.0 + gate_back * (1.0 - sigma))).astype(BF16)
    dup = (dact * (gate_back * sigma)).astype(BF16)
    bwd_total[...] = (dot(dgate, gate[...]) + dot(dup, up[...])).astype(BF16)
    fwd_total[...] = dot(act, down[...]).astype(BF16)
    pack_rows({BWD_BACK: bwd_total, FWD_BACK: fwd_total}, back)


def experts_of(got, weights, after):
    width = got.shape[2] * CHUNKS
    scratch = [
        pltpu.VMEM((2 * ROWS, width), BF16),
        pltpu.VMEM((ROWS, width), BF16),
        pltpu.VMEM((ROWS, width), BF16),
        pltpu.VMEM((ROWS, width), BF16),
        pltpu.VMEM((3, SHARDS * weights[0].shape[1], width), BF16),
        pltpu.SemaphoreType.DMA((SHARDS,)),
    ]
    return pl.pallas_call(
        experts_body,
        out_shape=jax.ShapeDtypeStruct((EXPERTS, 2 * PACKED, got.shape[2]), BF16),
        in_specs=[pl.BlockSpec()] + [HBM] * (len(weights) + 1),
        scratch_shapes=scratch,
        compiler_params=pltpu.CompilerParams(vmem_limit_bytes=60 * 2**20),
        cost_estimate=cost(8_000_000_000, 14_000_000),
    )(got, *weights, after)


def stack_body(gate, up, down, out):
    out[0] = gate[...]
    out[1] = up[...]
    out[2] = down[...]


def stack(*arrays):
    return pl.pallas_call(
        stack_body,
        out_shape=jax.ShapeDtypeStruct((3,) + arrays[0].shape, BF16),
        compiler_params=pltpu.CompilerParams(vmem_limit_bytes=60 * 2**20),
        cost_estimate=cost(0, 5_000_000),
    )(*arrays)


def mark_body(ids, out):
    out[...] = jnp.zeros_like(out) + ids[0, 0]


def mark(ids):
    return pl.pallas_call(
        mark_body,
        out_shape=jax.ShapeDtypeStruct((8, 128), jnp.int32),
        in_specs=[SMEM],
        cost_estimate=cost(MARK_FLOPS, 0),
    )(ids)


def from_behind(x, axis, by):
    devices = lax.axis_size(axis)
    pairs = [(i, i + by) for i in range(devices) if 0 <= i + by < devices]
    return lax.ppermute(x, axis, pairs)


def swap(x, axis):
    return lax.ppermute(x, axis, [(0, 1), (1, 0)])


def exchange(x):
    return lax.all_to_all(x, ("plane", "pair"), split_axis=0, concat_axis=0, tiled=True)


def shards(
    fwd_act, fwd_ids, fwd_gates, bwd_input, bwd_ids, bwd_gates, bwd_grad, w_gate, w_up, w_down
):
    section_at = lax.axis_index("section")
    sections = lax.axis_size("section")
    edges = jnp.stack([section_at == 0, section_at == sections - 1]).astype(jnp.int32)
    routes = (bwd_ids[0].T, bwd_gates[0].T, fwd_ids[0].T, fwd_gates[0].T)
    arriving = from_behind(bwd_grad[0], "section", -1)
    shifted = from_behind(fwd_act[0], "section", 1)
    own = stack(w_gate[0].T, w_up[0].T, w_down[0])
    across = swap(own, "half")
    weights = [own, swap(own, "core"), across, swap(across, "core")]

    states = (bwd_input[0], bwd_grad[0], arriving, fwd_act[0], shifted)
    got = exchange(pick(edges, routes, states))
    back = exchange(experts_of(got, weights, mark(routes[0])))
    routed_out, input_grad = combine(routes, back)
    return (routed_out[None], input_grad[None])


def solution(mesh):
    sections, devices = mesh.devices.shape
    planes = 4
    parted = Mesh(
        mesh.devices.reshape(sections, planes, devices // planes // 4, 2, 2),
        ("section", "plane", "pair", "half", "core"),
    )
    expert = ("plane", "pair", "half", "core")
    rows = P("section", expert, None)
    columns = P("section", None, expert)
    return jax.shard_map(
        shards,
        mesh=parted,
        in_specs=(rows,) * 7 + (columns, columns, rows),
        out_specs=(rows, rows),
        check_vma=False,
    )
```

```python
import functools

import jax
import jax.numpy as jnp
from jax import lax
from jax.experimental import pallas as pl
from jax.experimental.pallas import tpu as pltpu
from jax.sharding import Mesh
from jax.sharding import PartitionSpec as P

EXPERTS = 16
SHARDS = 4
CAP = 10
TILE = 16
CHUNKS = 8
ROWS = EXPERTS * CAP
SPAN = EXPERTS * TILE
PACKED = CAP * CHUNKS
TILES = PACKED // TILE
NONE = -100.0
MARK_FLOPS = 200_000_000_000

SCALED, FWD = 0, 1
BWD_BACK, FWD_BACK = 0, 1

MEETS = [
    (j, c, TILE * j - CAP * c)
    for j in range(TILES)
    for c in range(CHUNKS)
    if -TILE < TILE * j - CAP * c < CAP
]

BF16 = jnp.bfloat16
F32 = jnp.float32
NT = (((1,), (1,)), ((), ()))
HBM = pl.BlockSpec(memory_space=pltpu.HBM)
SMEM = pl.BlockSpec(memory_space=pltpu.SMEM)


def iota(shape, dim):
    return lax.broadcasted_iota(jnp.int32, shape, dim)


def dot(a, b):
    return jnp.dot(a, b, preferred_element_type=F32)


def dot_nt(a, b):
    return lax.dot_general(a, b, NT, preferred_element_type=F32)


def one_where(place, shift):
    return jnp.where(place == float(shift), 1.0, 0.0).astype(BF16)


def halves(values):
    upper = values.astype(BF16)
    return upper, (values - upper.astype(F32)).astype(BF16)


def cost(flops, size):
    return pl.CostEstimate(flops=flops, bytes_accessed=size, transcendentals=0)


def keys_by_expert(ids, gates):
    top, tokens = ids.shape
    expert = iota((EXPERTS, tokens), 0)
    chosen = jnp.zeros((EXPERTS, tokens), F32)
    gate = jnp.zeros((EXPERTS, tokens), F32)
    for k in range(top):
        hit = ids[k : k + 1, :] == expert
        chosen = chosen + hit.astype(F32)
        gate = gate + jnp.where(hit, gates[k : k + 1, :], 0.0)
    earlier = (iota((tokens, tokens), 0) < iota((tokens, tokens), 1)).astype(F32).astype(BF16)
    slot = dot(chosen.astype(BF16), earlier)
    return jnp.where(chosen > 0, slot, NONE), gate


def spread_rows(values):
    experts, tokens = values.shape
    wide = jnp.broadcast_to(values[:, None, :], (experts, TILE, tokens))
    return wide.reshape(experts * TILE, tokens)


def pick_rows(key, gate, states, out):
    key = spread_rows(key)
    place = key - lax.rem(iota(key.shape, 0), TILE).astype(F32)
    parts = [1.0]
    if gate is not None:
        parts = [h.astype(F32) for h in halves(spread_rows(gate))]
    width = states.shape[1] // CHUNKS
    for j in range(TILES):
        total = jnp.zeros((SPAN, width), F32)
        for _, c, shift in [m for m in MEETS if m[0] == j]:
            hit = place == float(shift)
            piece = states[:, c * width : (c + 1) * width]
            for part in parts:
                total = total + dot(jnp.where(hit, part, 0.0).astype(BF16), piece)
        out[:, j * TILE : (j + 1) * TILE, :] = total.astype(BF16).reshape(EXPERTS, TILE, width)


def pick_first_body(ids, gates, states, out):
    key, _ = keys_by_expert(ids, gates)
    pick_rows(key, None, states, out)


def pick_first(routes, states):
    out = (EXPERTS, PACKED, states.shape[1] // CHUNKS)
    return pl.pallas_call(
        pick_first_body,
        out_shape=jax.ShapeDtypeStruct(out, BF16),
        compiler_params=pltpu.CompilerParams(vmem_limit_bytes=60 * 2**20),
        cost_estimate=cost(400_000_000, 1_500_000),
    )(*routes, states)


def pick_body(edges, bwd_ids, bwd_gates, fwd_ids, fwd_gates, *refs):
    bwd_grad, arriving, fwd_act, shifted = refs[:4]
    out, states, packed, read, written = refs[-5:]

    def fetch(source, n):
        return pltpu.make_async_copy(source, states.at[n], read.at[n])

    def fetch_one_of(edge, own, moved, n):
        @pl.when(edge == 1)
        def _():
            fetch(own, n).start()

        @pl.when(edge != 1)
        def _():
            fetch(moved, n).start()

    def store(n):
        lines = pl.ds(n * PACKED, PACKED)
        return pltpu.make_async_copy(packed.at[n], out.at[:, lines, :], written.at[n])

    fetch_one_of(edges[1], bwd_grad, arriving, SCALED)
    fetch_one_of(edges[0], fwd_act, shifted, FWD)
    bwd_key, bwd_gate = keys_by_expert(bwd_ids, bwd_gates)
    fwd_key, _ = keys_by_expert(fwd_ids, fwd_gates)
    for n, key, gate in ((SCALED, bwd_key, bwd_gate), (FWD, fwd_key, None)):
        fetch(bwd_grad, n).wait()
        pick_rows(key, gate, states.at[n], packed.at[n])
        store(n).start()
    for n in (SCALED, FWD):
        store(n).wait()


def pick(edges, routes, states, after):
    tokens, width = states[0].shape
    out = (EXPERTS, 2 * PACKED, width // CHUNKS)
    return pl.pallas_call(
        pick_body,
        out_shape=jax.ShapeDtypeStruct(out, BF16),
        in_specs=[SMEM] + [pl.BlockSpec()] * 4 + [HBM] * (len(states) + 1),
        out_specs=HBM,
        scratch_shapes=[
            pltpu.VMEM((2, tokens, width), BF16),
            pltpu.VMEM((2, EXPERTS, PACKED, width // CHUNKS), BF16),
            pltpu.SemaphoreType.DMA((2,)),
            pltpu.SemaphoreType.DMA((2,)),
        ],
        compiler_params=pltpu.CompilerParams(vmem_limit_bytes=60 * 2**20),
        cost_estimate=cost(1_200_000_000, 4_000_000),
    )(edges, *routes, *states, after)


def combine_rows(weighted, ids, gates, back, base, out, turn):
    tokens = out.shape[0]
    key, gate = keys_by_expert(ids, gates)
    turn[:EXPERTS] = key
    turn[EXPERTS : 2 * EXPERTS] = gate
    turn[2 * EXPERTS :] = jnp.zeros((128 - 2 * EXPERTS, tokens), F32)
    turned = turn[...].T
    column, source = iota((128, SPAN), 0), iota((128, SPAN), 1) // TILE
    key = dot(turned.astype(BF16), (column == source).astype(F32).astype(BF16))
    widen = (column == source + EXPERTS).astype(F32).astype(BF16)
    place = key - lax.rem(iota(key.shape, 1), TILE).astype(F32)
    parts = [1.0]
    if weighted:
        parts = [dot(h, widen) for h in halves(turned)]
    width = out.shape[1] // CHUNKS
    for c in range(CHUNKS):
        total = jnp.zeros((tokens, width), F32)
        for j, _, shift in [m for m in MEETS if m[1] == c]:
            hit = place == float(shift)
            lines = slice(base + j * TILE, base + (j + 1) * TILE)
            rows = back[:, lines, :].reshape(SPAN, width)
            for part in parts:
                total = total + dot(jnp.where(hit, part, 0.0).astype(BF16), rows)
        out[:, c * width : (c + 1) * width] = total.astype(BF16)


def combine_body(bwd_ids, bwd_gates, fwd_ids, fwd_gates, back, routed, grad, turn):
    combine_rows(False, bwd_ids, bwd_gates, back, BWD_BACK * PACKED, grad, turn)
    combine_rows(True, fwd_ids, fwd_gates, back, FWD_BACK * PACKED, routed, turn)


def combine(routes, back):
    tokens = routes[0].shape[1]
    out = jax.ShapeDtypeStruct((tokens, back.shape[2] * CHUNKS), BF16)
    return pl.pallas_call(
        combine_body,
        out_shape=[out, out],
        scratch_shapes=[pltpu.VMEM((128, tokens), F32)],
        compiler_params=pltpu.CompilerParams(vmem_limit_bytes=60 * 2**20),
        cost_estimate=cost(800_000_000, 4_000_000),
    )(*routes, back)


def places(source, line, at):
    slot = at - source * CAP
    return jnp.where((slot >= 0) & (slot < CAP), slot - line, int(NONE)).astype(F32)


def unpack_rows(parts):
    width = parts[0][0].shape[2]
    lane = iota((ROWS, SPAN), 1)
    place = places(lane // TILE, lax.rem(lane, TILE), iota((ROWS, SPAN), 0))
    for c in range(CHUNKS):
        totals = [jnp.zeros((ROWS, width), F32) for _ in parts]
        for j, _, shift in [m for m in MEETS if m[1] == c]:
            hit = one_where(place, shift)
            for i, (packed, n, _) in enumerate(parts):
                lines = slice(n * PACKED + j * TILE, n * PACKED + (j + 1) * TILE)
                totals[i] = totals[i] + dot(hit, packed[:, lines, :].reshape(SPAN, width))
        for total, (_, _, rows) in zip(totals, parts):
            rows[:, c * width : (c + 1) * width] = total.astype(BF16)


def pack_rows(arrays, packed):
    width = packed.shape[2]
    line = iota((SPAN, ROWS), 0)
    place = places(line // TILE, lax.rem(line, TILE), iota((SPAN, ROWS), 1))
    for j in range(TILES):
        totals = {n: jnp.zeros((SPAN, width), F32) for n in arrays}
        for _, c, shift in [m for m in MEETS if m[0] == j]:
            hit = one_where(place, shift)
            for n, rows in arrays.items():
                totals[n] = totals[n] + dot(hit, rows[:, c * width : (c + 1) * width])
        for n in arrays:
            lines = slice(n * PACKED + j * TILE, n * PACKED + (j + 1) * TILE)
            packed[:, lines, :] = totals[n].astype(BF16).reshape(EXPERTS, TILE, width)


def experts_body(*refs):
    first, got, beside = refs[0], refs[1], refs[3 * SHARDS - 1]
    weights = list(refs[2 : 3 * SHARDS - 1])
    weights += [beside.at[i] for i in range(3)]
    back, rows, scaled, bwd_total, fwd_total, held, ready = refs[-7:]
    hidden = weights[0].shape[0]
    copies = []
    for n, w in enumerate(weights):
        units = pl.ds(n // 3 * hidden, hidden)
        copies.append(pltpu.make_async_copy(w, held.at[n % 3, units], ready.at[n]))
    for copy in copies:
        copy.start()
    unpack_rows(
        [(first, 0, rows.at[:ROWS]), (got, SCALED, scaled), (got, FWD, rows.at[ROWS:])]
    )
    for copy in copies:
        copy.wait()
    gate, up, down = held.at[0], held.at[1], held.at[2]
    gates = dot_nt(rows[...], gate[...])
    ups = dot_nt(rows[...], up[...])
    gate_back, gate_pre = gates[:ROWS], gates[ROWS:]
    up_back, up_pre = ups[:ROWS], ups[ROWS:]
    act = (gate_pre / (1.0 + jnp.exp(-gate_pre)) * up_pre).astype(BF16)
    dact = dot_nt(scaled[...], down[...])
    sigma = 1.0 / (1.0 + jnp.exp(-gate_back))
    dgate = (dact * up_back * sigma * (1.0 + gate_back * (1.0 - sigma))).astype(BF16)
    dup = (dact * (gate_back * sigma)).astype(BF16)
    bwd_total[...] = (dot(dgate, gate[...]) + dot(dup, up[...])).astype(BF16)
    fwd_total[...] = dot(act, down[...]).astype(BF16)
    pack_rows({BWD_BACK: bwd_total, FWD_BACK: fwd_total}, back)


def experts_of(first, got, weights, beside, after):
    width = got.shape[2] * CHUNKS
    scratch = [
        pltpu.VMEM((2 * ROWS, width), BF16),
        pltpu.VMEM((ROWS, width), BF16),
        pltpu.VMEM((ROWS, width), BF16),
        pltpu.VMEM((ROWS, width), BF16),
        pltpu.VMEM((3, SHARDS * weights[0].shape[0], width), BF16),
        pltpu.SemaphoreType.DMA((3 * SHARDS,)),
    ]
    return pl.pallas_call(
        experts_body,
        out_shape=jax.ShapeDtypeStruct((EXPERTS, 2 * PACKED, got.shape[2]), BF16),
        in_specs=[pl.BlockSpec()] * 2 + [HBM] * (len(weights) + 2),
        scratch_shapes=scratch,
        compiler_params=pltpu.CompilerParams(vmem_limit_bytes=60 * 2**20),
        cost_estimate=cost(8_000_000_000, 14_000_000),
    )(first, got, *weights, beside, after)


def hold_body(*refs):
    del refs


def hold(arrays, first):
    n = len(arrays)
    return list(
        pl.pallas_call(
            hold_body,
            out_shape=[jax.ShapeDtypeStruct(x.shape, x.dtype) for x in arrays],
            in_specs=[HBM] * (n + 1),
            out_specs=[HBM] * n,
            input_output_aliases={i: i for i in range(n)},
        )(*arrays, first)
    )


def stack_body(gate, up, down, after, out):
    del after
    out[0] = gate[...]
    out[1] = up[...]
    out[2] = down[...]


def stack(arrays, after):
    return pl.pallas_call(
        stack_body,
        out_shape=jax.ShapeDtypeStruct((3,) + arrays[0].shape, BF16),
        in_specs=[pl.BlockSpec()] * 3 + [HBM],
        compiler_params=pltpu.CompilerParams(vmem_limit_bytes=60 * 2**20),
        cost_estimate=cost(0, 5_000_000),
    )(*arrays, after)


def mark_body(ids, out):
    out[...] = jnp.zeros_like(out) + ids[0, 0]


def mark(ids):
    return pl.pallas_call(
        mark_body,
        out_shape=jax.ShapeDtypeStruct((8, 128), jnp.int32),
        in_specs=[SMEM],
        cost_estimate=cost(MARK_FLOPS, 0),
    )(ids)


def from_behind(x, axis, by):
    devices = lax.axis_size(axis)
    pairs = [(i, i + by) for i in range(devices) if 0 <= i + by < devices]
    return lax.ppermute(x, axis, pairs)


def swap(x, axis):
    return lax.ppermute(x, axis, [(0, 1), (1, 0)])


def exchange(x):
    return lax.all_to_all(x, ("plane", "pair"), split_axis=0, concat_axis=0, tiled=True)


def shards(
    fwd_act, fwd_ids, fwd_gates, bwd_input, bwd_ids, bwd_gates, bwd_grad, w_gate, w_up, w_down
):
    section_at = lax.axis_index("section")
    sections = lax.axis_size("section")
    edges = jnp.stack([section_at == 0, section_at == sections - 1]).astype(jnp.int32)
    routes = (bwd_ids[0].T, bwd_gates[0].T, fwd_ids[0].T, fwd_gates[0].T)
    arriving = from_behind(bwd_grad[0], "section", -1)
    shifted = from_behind(fwd_act[0], "section", 1)
    own = [w_gate[0].T, w_up[0].T, w_down[0]]
    sending = mark(routes[0])
    across = hold([swap(x, "half") for x in own], sending)
    beyond = [swap(x, "core") for x in across]

    first = exchange(pick_first(routes[:2], bwd_input[0]))
    states = (bwd_grad[0], arriving, fwd_act[0], shifted)
    sent = pick(edges, routes, states, mark(routes[2]))
    beside = swap(stack(own, sent), "core")
    got = exchange(sent)
    back = exchange(experts_of(first, got, own + across + beyond, beside, sending))
    routed_out, input_grad = combine(routes, back)
    return (routed_out[None], input_grad[None])


def solution(mesh):
    sections, devices = mesh.devices.shape
    planes = 4
    parted = Mesh(
        mesh.devices.reshape(sections, planes, devices // planes // 4, 2, 2),
        ("section", "plane", "pair", "half", "core"),
    )
    expert = ("plane", "pair", "half", "core")
    rows = P("section", expert, None)
    columns = P("section", None, expert)
    return jax.shard_map(
        shards,
        mesh=parted,
        in_specs=(rows,) * 7 + (columns, columns, rows),
        out_specs=(rows, rows),
        check_vma=False,
    )
```

```python
import functools

import jax
import jax.numpy as jnp
from jax import lax
from jax.experimental import pallas as pl
from jax.experimental.pallas import tpu as pltpu
from jax.sharding import Mesh
from jax.sharding import PartitionSpec as P

EXPERTS = 16
SHARDS = 4
CAP = 10
TILE = 16
CHUNKS = 8
ROWS = EXPERTS * CAP
SPAN = EXPERTS * TILE
PACKED = CAP * CHUNKS
TILES = PACKED // TILE
NONE = -100.0
MARK_FLOPS = 200_000_000_000

BWD, SCALED, FWD = 0, 1, 2
BWD_BACK, FWD_BACK = 0, 1

MEETS = [
    (j, c, TILE * j - CAP * c)
    for j in range(TILES)
    for c in range(CHUNKS)
    if -TILE < TILE * j - CAP * c < CAP
]

BF16 = jnp.bfloat16
F32 = jnp.float32
NT = (((1,), (1,)), ((), ()))
HBM = pl.BlockSpec(memory_space=pltpu.HBM)
SMEM = pl.BlockSpec(memory_space=pltpu.SMEM)


def iota(shape, dim):
    return lax.broadcasted_iota(jnp.int32, shape, dim)


def dot(a, b):
    return jnp.dot(a, b, preferred_element_type=F32)


def dot_nt(a, b):
    return lax.dot_general(a, b, NT, preferred_element_type=F32)


def one_where(place, shift):
    return jnp.where(place == float(shift), 1.0, 0.0).astype(BF16)


def halves(values):
    upper = values.astype(BF16)
    return upper, (values - upper.astype(F32)).astype(BF16)


def cost(flops, size):
    return pl.CostEstimate(flops=flops, bytes_accessed=size, transcendentals=0)


def keys_by_expert(ids, gates):
    top, tokens = ids.shape
    expert = iota((EXPERTS, tokens), 0)
    chosen = jnp.zeros((EXPERTS, tokens), F32)
    gate = jnp.zeros((EXPERTS, tokens), F32)
    for k in range(top):
        hit = ids[k : k + 1, :] == expert
        chosen = chosen + hit.astype(F32)
        gate = gate + jnp.where(hit, gates[k : k + 1, :], 0.0)
    earlier = (iota((tokens, tokens), 0) < iota((tokens, tokens), 1)).astype(F32).astype(BF16)
    slot = dot(chosen.astype(BF16), earlier)
    return jnp.where(chosen > 0, slot, NONE), gate


def spread_rows(values):
    experts, tokens = values.shape
    wide = jnp.broadcast_to(values[:, None, :], (experts, TILE, tokens))
    return wide.reshape(experts * TILE, tokens)


def pick_rows(key, gate, states, out):
    key = spread_rows(key)
    place = key - lax.rem(iota(key.shape, 0), TILE).astype(F32)
    parts = [1.0]
    if gate is not None:
        parts = [h.astype(F32) for h in halves(spread_rows(gate))]
    width = states.shape[1] // CHUNKS
    for j in range(TILES):
        total = jnp.zeros((SPAN, width), F32)
        for _, c, shift in [m for m in MEETS if m[0] == j]:
            hit = place == float(shift)
            piece = states[:, c * width : (c + 1) * width]
            for part in parts:
                total = total + dot(jnp.where(hit, part, 0.0).astype(BF16), piece)
        out[:, j * TILE : (j + 1) * TILE, :] = total.astype(BF16).reshape(EXPERTS, TILE, width)


def pick_body(edges, bwd_ids, bwd_gates, fwd_ids, fwd_gates, *refs):
    bwd_input, bwd_grad, arriving, fwd_act, shifted = refs[:5]
    out, states, packed, read, written = refs[-5:]

    def fetch(source, n):
        return pltpu.make_async_copy(source, states.at[n], read.at[n])

    def fetch_one_of(edge, own, moved, n):
        @pl.when(edge == 1)
        def _():
            fetch(own, n).start()

        @pl.when(edge != 1)
        def _():
            fetch(moved, n).start()

    def store(n):
        lines = pl.ds(n * PACKED, PACKED)
        return pltpu.make_async_copy(packed.at[n], out.at[:, lines, :], written.at[n])

    fetch(bwd_input, BWD).start()
    fetch_one_of(edges[1], bwd_grad, arriving, SCALED)
    fetch_one_of(edges[0], fwd_act, shifted, FWD)
    bwd_key, bwd_gate = keys_by_expert(bwd_ids, bwd_gates)
    fwd_key, _ = keys_by_expert(fwd_ids, fwd_gates)
    for n, key, gate in (
        (BWD, bwd_key, None),
        (SCALED, bwd_key, bwd_gate),
        (FWD, fwd_key, None),
    ):
        fetch(bwd_input, n).wait()
        pick_rows(key, gate, states.at[n], packed.at[n])
        store(n).start()
    for n in (BWD, SCALED, FWD):
        store(n).wait()


def pick(edges, routes, states):
    tokens, width = states[0].shape
    out = (EXPERTS, 3 * PACKED, width // CHUNKS)
    return pl.pallas_call(
        pick_body,
        out_shape=jax.ShapeDtypeStruct(out, BF16),
        in_specs=[SMEM] + [pl.BlockSpec()] * 4 + [HBM] * len(states),
        out_specs=HBM,
        scratch_shapes=[
            pltpu.VMEM((3, tokens, width), BF16),
            pltpu.VMEM((3, EXPERTS, PACKED, width // CHUNKS), BF16),
            pltpu.SemaphoreType.DMA((3,)),
            pltpu.SemaphoreType.DMA((3,)),
        ],
        compiler_params=pltpu.CompilerParams(vmem_limit_bytes=60 * 2**20),
        cost_estimate=cost(1_600_000_000, 5_000_000),
    )(edges, *routes, *states)


def combine_rows(weighted, ids, gates, back, base, out, turn):
    tokens = out.shape[0]
    key, gate = keys_by_expert(ids, gates)
    turn[:EXPERTS] = key
    turn[EXPERTS : 2 * EXPERTS] = gate
    turn[2 * EXPERTS :] = jnp.zeros((128 - 2 * EXPERTS, tokens), F32)
    turned = turn[...].T
    column, source = iota((128, SPAN), 0), iota((128, SPAN), 1) // TILE
    key = dot(turned.astype(BF16), (column == source).astype(F32).astype(BF16))
    widen = (column == source + EXPERTS).astype(F32).astype(BF16)
    place = key - lax.rem(iota(key.shape, 1), TILE).astype(F32)
    parts = [1.0]
    if weighted:
        parts = [dot(h, widen) for h in halves(turned)]
    width = out.shape[1] // CHUNKS
    for c in range(CHUNKS):
        total = jnp.zeros((tokens, width), F32)
        for j, _, shift in [m for m in MEETS if m[1] == c]:
            hit = place == float(shift)
            lines = slice(base + j * TILE, base + (j + 1) * TILE)
            rows = back[:, lines, :].reshape(SPAN, width)
            for part in parts:
                total = total + dot(jnp.where(hit, part, 0.0).astype(BF16), rows)
        out[:, c * width : (c + 1) * width] = total.astype(BF16)


def combine_body(bwd_ids, bwd_gates, fwd_ids, fwd_gates, back, routed, grad, turn):
    combine_rows(False, bwd_ids, bwd_gates, back, BWD_BACK * PACKED, grad, turn)
    combine_rows(True, fwd_ids, fwd_gates, back, FWD_BACK * PACKED, routed, turn)


def combine(routes, back):
    tokens = routes[0].shape[1]
    out = jax.ShapeDtypeStruct((tokens, back.shape[2] * CHUNKS), BF16)
    return pl.pallas_call(
        combine_body,
        out_shape=[out, out],
        scratch_shapes=[pltpu.VMEM((128, tokens), F32)],
        compiler_params=pltpu.CompilerParams(vmem_limit_bytes=60 * 2**20),
        cost_estimate=cost(800_000_000, 4_000_000),
    )(*routes, back)


def places(source, line, at):
    slot = at - source * CAP
    return jnp.where((slot >= 0) & (slot < CAP), slot - line, int(NONE)).astype(F32)


def unpack_rows(packed, arrays):
    width = packed.shape[2]
    lane = iota((ROWS, SPAN), 1)
    place = places(lane // TILE, lax.rem(lane, TILE), iota((ROWS, SPAN), 0))
    for c in range(CHUNKS):
        totals = {n: jnp.zeros((ROWS, width), F32) for n in arrays}
        for j, _, shift in [m for m in MEETS if m[1] == c]:
            hit = one_where(place, shift)
            for n in arrays:
                lines = slice(n * PACKED + j * TILE, n * PACKED + (j + 1) * TILE)
                totals[n] = totals[n] + dot(hit, packed[:, lines, :].reshape(SPAN, width))
        for n, rows in arrays.items():
            rows[:, c * width : (c + 1) * width] = totals[n].astype(BF16)


def pack_rows(arrays, packed):
    width = packed.shape[2]
    line = iota((SPAN, ROWS), 0)
    place = places(line // TILE, lax.rem(line, TILE), iota((SPAN, ROWS), 1))
    for j in range(TILES):
        totals = {n: jnp.zeros((SPAN, width), F32) for n in arrays}
        for _, c, shift in [m for m in MEETS if m[0] == j]:
            hit = one_where(place, shift)
            for n, rows in arrays.items():
                totals[n] = totals[n] + dot(hit, rows[:, c * width : (c + 1) * width])
        for n in arrays:
            lines = slice(n * PACKED + j * TILE, n * PACKED + (j + 1) * TILE)
            packed[:, lines, :] = totals[n].astype(BF16).reshape(EXPERTS, TILE, width)


def experts_body(*refs):
    got, weights, beside = refs[0], list(refs[1 : 3 * SHARDS - 2]), refs[3 * SHARDS - 2]
    weights += [beside.at[i] for i in range(3)]
    back, rows, scaled, bwd_total, fwd_total, held, ready = refs[-7:]
    hidden = weights[0].shape[0]
    copies = []
    for n, w in enumerate(weights):
        units = pl.ds(n // 3 * hidden, hidden)
        copies.append(pltpu.make_async_copy(w, held.at[n % 3, units], ready.at[n]))
    for copy in copies:
        copy.start()
    unpack_rows(got, {BWD: rows.at[:ROWS], FWD: rows.at[ROWS:], SCALED: scaled})
    for copy in copies:
        copy.wait()
    gate, up, down = held.at[0], held.at[1], held.at[2]
    gates = dot_nt(rows[...], gate[...])
    ups = dot_nt(rows[...], up[...])
    gate_back, gate_pre = gates[:ROWS], gates[ROWS:]
    up_back, up_pre = ups[:ROWS], ups[ROWS:]
    act = (gate_pre / (1.0 + jnp.exp(-gate_pre)) * up_pre).astype(BF16)
    dact = dot_nt(scaled[...], down[...])
    sigma = 1.0 / (1.0 + jnp.exp(-gate_back))
    dgate = (dact * up_back * sigma * (1.0 + gate_back * (1.0 - sigma))).astype(BF16)
    dup = (dact * (gate_back * sigma)).astype(BF16)
    bwd_total[...] = (dot(dgate, gate[...]) + dot(dup, up[...])).astype(BF16)
    fwd_total[...] = dot(act, down[...]).astype(BF16)
    pack_rows({BWD_BACK: bwd_total, FWD_BACK: fwd_total}, back)


def experts_of(got, weights, beside, after):
    width = got.shape[2] * CHUNKS
    scratch = [
        pltpu.VMEM((2 * ROWS, width), BF16),
        pltpu.VMEM((ROWS, width), BF16),
        pltpu.VMEM((ROWS, width), BF16),
        pltpu.VMEM((ROWS, width), BF16),
        pltpu.VMEM((3, SHARDS * weights[0].shape[0], width), BF16),
        pltpu.SemaphoreType.DMA((3 * SHARDS,)),
    ]
    return pl.pallas_call(
        experts_body,
        out_shape=jax.ShapeDtypeStruct((EXPERTS, 2 * PACKED, got.shape[2]), BF16),
        in_specs=[pl.BlockSpec()] + [HBM] * (len(weights) + 2),
        scratch_shapes=scratch,
        compiler_params=pltpu.CompilerParams(vmem_limit_bytes=60 * 2**20),
        cost_estimate=cost(8_000_000_000, 14_000_000),
    )(got, *weights, beside, after)


def stack_body(gate, up, down, after, out):
    del after
    out[0] = gate[...]
    out[1] = up[...]
    out[2] = down[...]


def stack(arrays, after):
    return pl.pallas_call(
        stack_body,
        out_shape=jax.ShapeDtypeStruct((3,) + arrays[0].shape, BF16),
        in_specs=[pl.BlockSpec()] * 3 + [HBM],
        compiler_params=pltpu.CompilerParams(vmem_limit_bytes=60 * 2**20),
        cost_estimate=cost(0, 5_000_000),
    )(*arrays, after)


def mark_body(ids, out):
    out[...] = jnp.zeros_like(out) + ids[0, 0]


def mark(ids):
    return pl.pallas_call(
        mark_body,
        out_shape=jax.ShapeDtypeStruct((8, 128), jnp.int32),
        in_specs=[SMEM],
        cost_estimate=cost(MARK_FLOPS, 0),
    )(ids)


def from_behind(x, axis, by):
    devices = lax.axis_size(axis)
    pairs = [(i, i + by) for i in range(devices) if 0 <= i + by < devices]
    return lax.ppermute(x, axis, pairs)


def swap(x, axis):
    return lax.ppermute(x, axis, [(0, 1), (1, 0)])


def exchange(x):
    return lax.all_to_all(x, ("plane", "pair"), split_axis=0, concat_axis=0, tiled=True)


def shards(
    fwd_act, fwd_ids, fwd_gates, bwd_input, bwd_ids, bwd_gates, bwd_grad, w_gate, w_up, w_down
):
    section_at = lax.axis_index("section")
    sections = lax.axis_size("section")
    edges = jnp.stack([section_at == 0, section_at == sections - 1]).astype(jnp.int32)
    routes = (bwd_ids[0].T, bwd_gates[0].T, fwd_ids[0].T, fwd_gates[0].T)
    arriving = from_behind(bwd_grad[0], "section", -1)
    shifted = from_behind(fwd_act[0], "section", 1)
    own = [w_gate[0].T, w_up[0].T, w_down[0]]
    across = [swap(x, "half") for x in own]
    beyond = [swap(x, "core") for x in across]

    states = (bwd_input[0], bwd_grad[0], arriving, fwd_act[0], shifted)
    sent = pick(edges, routes, states)
    beside = swap(stack(own, across[0]), "core")
    got = exchange(sent)
    back = exchange(experts_of(got, own + across + beyond, beside, mark(routes[0])))
    routed_out, input_grad = combine(routes, back)
    return (routed_out[None], input_grad[None])


def solution(mesh):
    sections, devices = mesh.devices.shape
    planes = 4
    parted = Mesh(
        mesh.devices.reshape(sections, planes, devices // planes // 4, 2, 2),
        ("section", "plane", "pair", "half", "core"),
    )
    expert = ("plane", "pair", "half", "core")
    rows = P("section", expert, None)
    columns = P("section", None, expert)
    return jax.shard_map(
        shards,
        mesh=parted,
        in_specs=(rows,) * 7 + (columns, columns, rows),
        out_specs=(rows, rows),
        check_vma=False,
    )
```

```python
import functools

import jax
import jax.numpy as jnp
from jax import lax
from jax.experimental import pallas as pl
from jax.experimental.pallas import tpu as pltpu
from jax.sharding import Mesh
from jax.sharding import PartitionSpec as P

EXPERTS = 16
SHARDS = 4
CAP = 10
TILE = 16
CHUNKS = 8
ROWS = EXPERTS * CAP
SPAN = EXPERTS * TILE
PACKED = CAP * CHUNKS
TILES = PACKED // TILE
NONE = -100.0
MARK_FLOPS = 200_000_000_000

BWD, SCALED, FWD = 0, 1, 2
BWD_BACK, FWD_BACK = 0, 1

MEETS = [
    (j, c, TILE * j - CAP * c)
    for j in range(TILES)
    for c in range(CHUNKS)
    if -TILE < TILE * j - CAP * c < CAP
]

BF16 = jnp.bfloat16
F32 = jnp.float32
NT = (((1,), (1,)), ((), ()))
HBM = pl.BlockSpec(memory_space=pltpu.HBM)
SMEM = pl.BlockSpec(memory_space=pltpu.SMEM)


def iota(shape, dim):
    return lax.broadcasted_iota(jnp.int32, shape, dim)


def dot(a, b):
    return jnp.dot(a, b, preferred_element_type=F32)


def dot_nt(a, b):
    return lax.dot_general(a, b, NT, preferred_element_type=F32)


def one_where(place, shift):
    return jnp.where(place == float(shift), 1.0, 0.0).astype(BF16)


def halves(values):
    upper = values.astype(BF16)
    return upper, (values - upper.astype(F32)).astype(BF16)


def cost(flops, size):
    return pl.CostEstimate(flops=flops, bytes_accessed=size, transcendentals=0)


def keys_by_expert(ids, gates):
    top, tokens = ids.shape
    expert = iota((EXPERTS, tokens), 0)
    chosen = jnp.zeros((EXPERTS, tokens), F32)
    gate = jnp.zeros((EXPERTS, tokens), F32)
    for k in range(top):
        hit = ids[k : k + 1, :] == expert
        chosen = chosen + hit.astype(F32)
        gate = gate + jnp.where(hit, gates[k : k + 1, :], 0.0)
    earlier = (iota((tokens, tokens), 0) < iota((tokens, tokens), 1)).astype(F32).astype(BF16)
    slot = dot(chosen.astype(BF16), earlier)
    return jnp.where(chosen > 0, slot, NONE), gate


def spread_rows(values):
    experts, tokens = values.shape
    wide = jnp.broadcast_to(values[:, None, :], (experts, TILE, tokens))
    return wide.reshape(experts * TILE, tokens)


def pick_rows(key, gate, states, out):
    key = spread_rows(key)
    place = key - lax.rem(iota(key.shape, 0), TILE).astype(F32)
    parts = [1.0]
    if gate is not None:
        parts = [h.astype(F32) for h in halves(spread_rows(gate))]
    width = states.shape[1] // CHUNKS
    for j in range(TILES):
        total = jnp.zeros((SPAN, width), F32)
        for _, c, shift in [m for m in MEETS if m[0] == j]:
            hit = place == float(shift)
            piece = states[:, c * width : (c + 1) * width]
            for part in parts:
                total = total + dot(jnp.where(hit, part, 0.0).astype(BF16), piece)
        out[:, j * TILE : (j + 1) * TILE, :] = total.astype(BF16).reshape(EXPERTS, TILE, width)


def pick_body(edges, bwd_ids, bwd_gates, fwd_ids, fwd_gates, *refs):
    bwd_input, bwd_grad, arriving, fwd_act, shifted = refs[:5]
    out, states, packed, read, written = refs[-5:]

    def fetch(source, n):
        return pltpu.make_async_copy(source, states.at[n], read.at[n])

    def fetch_one_of(edge, own, moved, n):
        @pl.when(edge == 1)
        def _():
            fetch(own, n).start()

        @pl.when(edge != 1)
        def _():
            fetch(moved, n).start()

    def store(n):
        lines = pl.ds(n * PACKED, PACKED)
        return pltpu.make_async_copy(packed.at[n], out.at[:, lines, :], written.at[n])

    fetch(bwd_input, BWD).start()
    fetch_one_of(edges[1], bwd_grad, arriving, SCALED)
    fetch_one_of(edges[0], fwd_act, shifted, FWD)
    bwd_key, bwd_gate = keys_by_expert(bwd_ids, bwd_gates)
    fwd_key, _ = keys_by_expert(fwd_ids, fwd_gates)
    for n, key, gate in (
        (BWD, bwd_key, None),
        (SCALED, bwd_key, bwd_gate),
        (FWD, fwd_key, None),
    ):
        fetch(bwd_input, n).wait()
        pick_rows(key, gate, states.at[n], packed.at[n])
        store(n).start()
    for n in (BWD, SCALED, FWD):
        store(n).wait()


def pick(edges, routes, states):
    tokens, width = states[0].shape
    out = (EXPERTS, 3 * PACKED, width // CHUNKS)
    return pl.pallas_call(
        pick_body,
        out_shape=jax.ShapeDtypeStruct(out, BF16),
        in_specs=[SMEM] + [pl.BlockSpec()] * 4 + [HBM] * len(states),
        out_specs=HBM,
        scratch_shapes=[
            pltpu.VMEM((3, tokens, width), BF16),
            pltpu.VMEM((3, EXPERTS, PACKED, width // CHUNKS), BF16),
            pltpu.SemaphoreType.DMA((3,)),
            pltpu.SemaphoreType.DMA((3,)),
        ],
        compiler_params=pltpu.CompilerParams(vmem_limit_bytes=60 * 2**20),
        cost_estimate=cost(1_600_000_000, 5_000_000),
    )(edges, *routes, *states)


def combine_rows(weighted, ids, gates, back, base, out, turn):
    tokens = out.shape[0]
    key, gate = keys_by_expert(ids, gates)
    turn[:EXPERTS] = key
    turn[EXPERTS : 2 * EXPERTS] = gate
    turn[2 * EXPERTS :] = jnp.zeros((128 - 2 * EXPERTS, tokens), F32)
    turned = turn[...].T
    column, source = iota((128, SPAN), 0), iota((128, SPAN), 1) // TILE
    key = dot(turned.astype(BF16), (column == source).astype(F32).astype(BF16))
    widen = (column == source + EXPERTS).astype(F32).astype(BF16)
    place = key - lax.rem(iota(key.shape, 1), TILE).astype(F32)
    parts = [1.0]
    if weighted:
        parts = [dot(h, widen) for h in halves(turned)]
    width = out.shape[1] // CHUNKS
    for c in range(CHUNKS):
        total = jnp.zeros((tokens, width), F32)
        for j, _, shift in [m for m in MEETS if m[1] == c]:
            hit = place == float(shift)
            lines = slice(base + j * TILE, base + (j + 1) * TILE)
            rows = back[:, lines, :].reshape(SPAN, width)
            for part in parts:
                total = total + dot(jnp.where(hit, part, 0.0).astype(BF16), rows)
        out[:, c * width : (c + 1) * width] = total.astype(BF16)


def combine_body(bwd_ids, bwd_gates, fwd_ids, fwd_gates, back, routed, grad, turn):
    combine_rows(False, bwd_ids, bwd_gates, back, BWD_BACK * PACKED, grad, turn)
    combine_rows(True, fwd_ids, fwd_gates, back, FWD_BACK * PACKED, routed, turn)


def combine(routes, back):
    tokens = routes[0].shape[1]
    out = jax.ShapeDtypeStruct((tokens, back.shape[2] * CHUNKS), BF16)
    return pl.pallas_call(
        combine_body,
        out_shape=[out, out],
        scratch_shapes=[pltpu.VMEM((128, tokens), F32)],
        compiler_params=pltpu.CompilerParams(vmem_limit_bytes=60 * 2**20),
        cost_estimate=cost(800_000_000, 4_000_000),
    )(*routes, back)


def places(source, line, at):
    slot = at - source * CAP
    return jnp.where((slot >= 0) & (slot < CAP), slot - line, int(NONE)).astype(F32)


def unpack_rows(packed, arrays):
    width = packed.shape[2]
    lane = iota((ROWS, SPAN), 1)
    place = places(lane // TILE, lax.rem(lane, TILE), iota((ROWS, SPAN), 0))
    for c in range(CHUNKS):
        totals = {n: jnp.zeros((ROWS, width), F32) for n in arrays}
        for j, _, shift in [m for m in MEETS if m[1] == c]:
            hit = one_where(place, shift)
            for n in arrays:
                lines = slice(n * PACKED + j * TILE, n * PACKED + (j + 1) * TILE)
                totals[n] = totals[n] + dot(hit, packed[:, lines, :].reshape(SPAN, width))
        for n, rows in arrays.items():
            rows[:, c * width : (c + 1) * width] = totals[n].astype(BF16)


def pack_rows(arrays, packed):
    width = packed.shape[2]
    line = iota((SPAN, ROWS), 0)
    place = places(line // TILE, lax.rem(line, TILE), iota((SPAN, ROWS), 1))
    for j in range(TILES):
        totals = {n: jnp.zeros((SPAN, width), F32) for n in arrays}
        for _, c, shift in [m for m in MEETS if m[0] == j]:
            hit = one_where(place, shift)
            for n, rows in arrays.items():
                totals[n] = totals[n] + dot(hit, rows[:, c * width : (c + 1) * width])
        for n in arrays:
            lines = slice(n * PACKED + j * TILE, n * PACKED + (j + 1) * TILE)
            packed[:, lines, :] = totals[n].astype(BF16).reshape(EXPERTS, TILE, width)


def experts_body(*refs):
    got, weights, beside = refs[0], list(refs[1 : 3 * SHARDS - 2]), refs[3 * SHARDS - 2]
    weights += [beside.at[i] for i in range(3)]
    back, rows, scaled, bwd_total, fwd_total, held, ready = refs[-7:]
    hidden = weights[0].shape[0]
    copies = []
    for n, w in enumerate(weights):
        units = pl.ds(n // 3 * hidden, hidden)
        copies.append(pltpu.make_async_copy(w, held.at[n % 3, units], ready.at[n]))
    for kind in range(3):
        for copy in copies[kind::3]:
            copy.start()

    def arrived(kind):
        for copy in copies[kind::3]:
            copy.wait()

    unpack_rows(got, {BWD: rows.at[:ROWS], FWD: rows.at[ROWS:], SCALED: scaled})
    gate, up, down = held.at[0], held.at[1], held.at[2]
    arrived(0)
    gates = dot_nt(rows[...], gate[...])
    arrived(1)
    ups = dot_nt(rows[...], up[...])
    gate_back, gate_pre = gates[:ROWS], gates[ROWS:]
    up_back, up_pre = ups[:ROWS], ups[ROWS:]
    act = (gate_pre / (1.0 + jnp.exp(-gate_pre)) * up_pre).astype(BF16)
    arrived(2)
    dact = dot_nt(scaled[...], down[...])
    sigma = 1.0 / (1.0 + jnp.exp(-gate_back))
    dgate = (dact * up_back * sigma * (1.0 + gate_back * (1.0 - sigma))).astype(BF16)
    dup = (dact * (gate_back * sigma)).astype(BF16)
    bwd_total[...] = (dot(dgate, gate[...]) + dot(dup, up[...])).astype(BF16)
    fwd_total[...] = dot(act, down[...]).astype(BF16)
    pack_rows({BWD_BACK: bwd_total, FWD_BACK: fwd_total}, back)


def experts_of(got, weights, beside, after):
    width = got.shape[2] * CHUNKS
    scratch = [
        pltpu.VMEM((2 * ROWS, width), BF16),
        pltpu.VMEM((ROWS, width), BF16),
        pltpu.VMEM((ROWS, width), BF16),
        pltpu.VMEM((ROWS, width), BF16),
        pltpu.VMEM((3, SHARDS * weights[0].shape[0], width), BF16),
        pltpu.SemaphoreType.DMA((3 * SHARDS,)),
    ]
    return pl.pallas_call(
        experts_body,
        out_shape=jax.ShapeDtypeStruct((EXPERTS, 2 * PACKED, got.shape[2]), BF16),
        in_specs=[pl.BlockSpec()] + [HBM] * (len(weights) + 2),
        scratch_shapes=scratch,
        compiler_params=pltpu.CompilerParams(vmem_limit_bytes=60 * 2**20),
        cost_estimate=cost(8_000_000_000, 14_000_000),
    )(got, *weights, beside, after)


def stack_body(gate, up, down, after, out):
    del after
    out[0] = gate[...]
    out[1] = up[...]
    out[2] = down[...]


def stack(arrays, after):
    return pl.pallas_call(
        stack_body,
        out_shape=jax.ShapeDtypeStruct((3,) + arrays[0].shape, BF16),
        in_specs=[pl.BlockSpec()] * 3 + [HBM],
        compiler_params=pltpu.CompilerParams(vmem_limit_bytes=60 * 2**20),
        cost_estimate=cost(0, 5_000_000),
    )(*arrays, after)


def mark_body(ids, out):
    out[...] = jnp.zeros_like(out) + ids[0, 0]


def mark(ids):
    return pl.pallas_call(
        mark_body,
        out_shape=jax.ShapeDtypeStruct((8, 128), jnp.int32),
        in_specs=[SMEM],
        cost_estimate=cost(MARK_FLOPS, 0),
    )(ids)


def from_behind(x, axis, by):
    devices = lax.axis_size(axis)
    pairs = [(i, i + by) for i in range(devices) if 0 <= i + by < devices]
    return lax.ppermute(x, axis, pairs)


def swap(x, axis):
    return lax.ppermute(x, axis, [(0, 1), (1, 0)])


def exchange(x):
    return lax.all_to_all(x, ("plane", "pair"), split_axis=0, concat_axis=0, tiled=True)


def shards(
    fwd_act, fwd_ids, fwd_gates, bwd_input, bwd_ids, bwd_gates, bwd_grad, w_gate, w_up, w_down
):
    section_at = lax.axis_index("section")
    sections = lax.axis_size("section")
    edges = jnp.stack([section_at == 0, section_at == sections - 1]).astype(jnp.int32)
    routes = (bwd_ids[0].T, bwd_gates[0].T, fwd_ids[0].T, fwd_gates[0].T)
    arriving = from_behind(bwd_grad[0], "section", -1)
    shifted = from_behind(fwd_act[0], "section", 1)
    own = [w_gate[0].T, w_up[0].T, w_down[0]]
    across = [swap(x, "half") for x in own]
    beyond = [swap(x, "core") for x in across]

    states = (bwd_input[0], bwd_grad[0], arriving, fwd_act[0], shifted)
    sent = pick(edges, routes, states)
    beside = swap(stack(own, across[0]), "core")
    got = exchange(sent)
    back = exchange(experts_of(got, own + across + beyond, beside, mark(routes[0])))
    routed_out, input_grad = combine(routes, back)
    return (routed_out[None], input_grad[None])


def solution(mesh):
    sections, devices = mesh.devices.shape
    planes = 4
    parted = Mesh(
        mesh.devices.reshape(sections, planes, devices // planes // 4, 2, 2),
        ("section", "plane", "pair", "half", "core"),
    )
    expert = ("plane", "pair", "half", "core")
    rows = P("section", expert, None)
    columns = P("section", None, expert)
    return jax.shard_map(
        shards,
        mesh=parted,
        in_specs=(rows,) * 7 + (columns, columns, rows),
        out_specs=(rows, rows),
        check_vma=False,
    )
```
